32 devices in a mesh: section: 2 (over core), dp: 4 (over z), tensor: 4 (over y, x).
Axes of the slice: x: 2, y: 2, z: 4, core: 2. Of those that a mesh axis runs over, the one named last changes fastest.
Arguments:
- inputs: bfloat16 [2, 4096, 768], P(None, ('dp', 'tensor')), may hold values from -6 to 6
- cotangent: bfloat16 [2, 4096, 768], P(None, ('dp', 'tensor')), may hold values from -6 to 6
- seq_lengths: int32 [2, 4, 8], P(None, 'dp'), may hold values from 0 to 1024, as said below
- norm_gain: float32 [2, 2, 768], P('section'), may hold values from 0.25 to 1.75
- norm_shift: float32 [2, 2, 768], P('section'), may hold values from -1 to 1
- w_qkv: bfloat16 [2, 3, 768, 768], P('section', None, 'dp', 'tensor'), may hold values from -0.21875 to 0.21875
- b_qv: float32 [2, 2, 768], P('section', None, 'tensor'), may hold values from -1.5 to 1.5
- w_out: bfloat16 [2, 768, 768], P('section', 'tensor', 'dp'), may hold values from -0.875 to 0.875
- b_out: float32 [2, 768], P('section'), may hold values from -1 to 1
- w_up: bfloat16 [2, 768, 3072], P('section', 'dp', 'tensor'), may hold values from -0.21875 to 0.21875
- b_up: float32 [2, 3072], P('section', 'tensor'), may hold values from -1.5 to 1.5
- w_down: bfloat16 [2, 3072, 768], P('section', 'tensor', 'dp'), may hold values from -0.15625 to 0.15625
- b_down: float32 [2, 768], P('section'), may hold values from -1 to 1
Outputs:
- layer_out: bfloat16 [2, 2, 4096, 768], P('section', None, ('dp', 'tensor'))
- input_grad: bfloat16 [2, 2, 4096, 768], P('section', None, ('dp', 'tensor'))
- grad_norm_gain: float32 [2, 2, 768], P('section')
- grad_norm_shift: float32 [2, 2, 768], P('section')
- grad_w_qkv: float32 [2, 3, 768, 768], P('section', None, 'dp', 'tensor')
- grad_b_qv: float32 [2, 2, 768], P('section', None, 'tensor')
- grad_w_out: float32 [2, 768, 768], P('section', 'tensor', 'dp')
- grad_b_out: float32 [2, 768], P('section')
- grad_w_up: float32 [2, 768, 3072], P('section', 'dp', 'tensor')
- grad_b_up: float32 [2, 3072], P('section', 'tensor')
- grad_w_down: float32 [2, 3072, 768], P('section', 'tensor', 'dp')
- grad_b_down: float32 [2, 768], P('section')
The draws below stay inside these ranges and needn't reach their ends.
Inputs may be any that keep to these rules, and one draw needn't show every extreme that they name: `seq_lengths`: in each micro-batch and data shard the sequences fill the slots from the first; a slot of length 0 holds no sequence; the lengths of one micro-batch on one data shard add up to at most 1024, exactly 1024 on some shard, and some sequence has length 1024.
All inputs are finite; a program needn't handle non-finite values.
Results may differ from the reference program's by a relative error of at most 0.02.
Values may be sent and summed in bfloat16 or wider, within the bound.
No kernel may reach another device: no remote copies, remote signals or barrier semaphores. Data moves between devices by JAX's collectives and lax.ppermute only.
A program may use at most 192 MiB of HBM per device.

```python
import jax
import jax.numpy as jnp
from jax import lax

HEADS = 12
HD = 64
D = 768
FF = 3072
ROWS = 1024
MAXLEN = 1024
SLOTS = 8
MICRO = 2
LAYERS = 2
TOKENS = 4096


def draw_seq_lengths(key, part):
    key = jax.random.fold_in(key, 11)
    shards = TOKENS // ROWS
    groups = MICRO * shards
    key_len, key_cap, key_pick = jax.random.split(key, 3)
    raw_lengths = jax.random.randint(key_len, (groups, SLOTS), MAXLEN // 4, MAXLEN + 1)
    capacity = jax.random.randint(key_cap, (groups,), ROWS // 2, ROWS + 1)
    chosen = jax.random.randint(key_pick, (), 0, groups)
    group_ids = jnp.arange(groups)
    first_slot = jnp.where(group_ids == chosen, MAXLEN, raw_lengths[:, 0])
    raw_lengths = raw_lengths.at[:, 0].set(first_slot)
    capacity = jnp.where(group_ids == chosen, ROWS, capacity)
    seq_ends = jnp.minimum(jnp.cumsum(raw_lengths, axis=1), capacity[:, None])
    seq_starts = jnp.concatenate([jnp.zeros((groups, 1), seq_ends.dtype), seq_ends[:, :-1]], axis=1)
    return (seq_ends - seq_starts).reshape(MICRO, shards, SLOTS).astype(jnp.int32)


def block_scale(rng, dims, cuts, least, largest):
    factor_of, own = 1.0, jax.random.fold_in(rng, 6)
    for dim, shards_of in cuts:
        draws = jnp.exp(jax.random.uniform(jax.random.fold_in(own, dim), (shards_of,), jnp.float32, least / len(cuts), largest / len(cuts)))
        factor_of = factor_of * jnp.repeat(draws, dims[dim] // shards_of).reshape([-1 if axis == dim else 1 for axis in range(len(dims))])
    return factor_of


def gaussian(key, shape, spread, limit, cuts=(), kind=jnp.bfloat16):
    result = spread * jax.random.normal(key, shape, jnp.float32)
    if cuts:
        result = result * block_scale(key, shape, cuts, -0.22, 0.18)
    return jnp.clip(result, -limit, limit).astype(kind)


def setup_inputs(seed: int = 0) -> dict:
    streams_of = jax.random.split(jax.random.key(seed), 14)
    return {
        "inputs": gaussian(streams_of[0], (MICRO, TOKENS, D), 1.0, 6.0, ((1, 16),)),
        "cotangent": gaussian(streams_of[1], (MICRO, TOKENS, D), 1.0, 6.0, ((1, 16),)),
        "seq_lengths": draw_seq_lengths(jax.random.fold_in(streams_of[13], 71), 0),
        "norm_gain": jnp.clip(1.0 + 0.15 * jax.random.normal(streams_of[3], (LAYERS, 2, D), jnp.float32), 0.25, 1.75),
        "norm_shift": gaussian(streams_of[4], (LAYERS, 2, D), 0.2, 1.0, ((0, 2),), jnp.float32),
        "w_qkv": gaussian(streams_of[5], (LAYERS, 3, D, D), D ** -0.5, 0.21875, ((0, 2), (2, 4), (3, 4))),
        "b_qv": gaussian(streams_of[6], (LAYERS, 2, D), 0.3, 1.5, ((0, 2), (2, 4)), jnp.float32),
        "w_out": gaussian(streams_of[7], (LAYERS, D, D), (D // 16) ** -0.5, 0.875, ((0, 2), (1, 4), (2, 4))),
        "b_out": gaussian(streams_of[8], (LAYERS, D), 0.2, 1.0, ((0, 2),), jnp.float32),
        "w_up": gaussian(streams_of[9], (LAYERS, D, FF), D ** -0.5, 0.21875, ((0, 2), (1, 4), (2, 4))),
        "b_up": gaussian(streams_of[10], (LAYERS, FF), 0.3, 1.5, ((0, 2), (1, 4)), jnp.float32),
        "w_down": gaussian(streams_of[11], (LAYERS, FF, D), (FF // 2) ** -0.5, 0.15625, ((0, 2), (1, 4), (2, 4))),
        "b_down": gaussian(streams_of[12], (LAYERS, D), 0.2, 1.0, ((0, 2),), jnp.float32),
    }


@jax.custom_vjp
def low(v):
    return lax.optimization_barrier(v.astype(jnp.bfloat16)).astype(jnp.float32)

@jax.custom_vjp
def low_back(v):
    return v

def low_keep(v):
    return (low(v), None)

def low_pass(kept, grad):
    return (grad,)

def back_keep(v):
    return (v, None)

def back_low(kept, grad):
    return (low(grad),)
low.defvjp(low_keep, low_pass)
low_back.defvjp(back_keep, back_low)

def norm_rows(values, norm_scale, norm_bias):
    row_mean = lax.optimization_barrier(jnp.mean(values, axis=-1, keepdims=True))
    centred = values - row_mean
    row_var = lax.optimization_barrier(jnp.mean(centred * centred, axis=-1, keepdims=True))
    return centred * lax.rsqrt(row_var + 1e-05) * norm_scale + norm_bias

def segments_of(lengths, total_rows):
    seq_ends = jnp.cumsum(lengths).astype(jnp.int32)
    places = jnp.arange(total_rows, dtype=jnp.int32)
    labels = lax.optimization_barrier(jnp.sum((places[:, None] >= seq_ends[None, :]).astype(jnp.int32), axis=1)).astype(jnp.int32)
    inside = places < seq_ends[-1]
    return (jnp.where(inside, labels, lengths.shape[0] + places).astype(jnp.int32), inside)

def dense(left, right):
    return jnp.dot(left, right, precision=lax.Precision.HIGHEST)

def attend(query, keys, values, labels):
    total_rows = query.shape[0]
    places = jnp.arange(total_rows, dtype=jnp.int32)
    allowed = (labels[:, None] == labels[None, :]) & (places[:, None] >= places[None, :])
    scores = low_back(jnp.einsum('qhd,khd->hqk', query, keys, precision=lax.Precision.HIGHEST))
    scores = jnp.where(allowed[None], scores, -1000000000.0)
    row_max = lax.optimization_barrier(jnp.max(scores, axis=-1, keepdims=True))
    weights = jnp.exp(scores - row_max)
    probs = low(weights / lax.optimization_barrier(jnp.sum(weights, axis=-1, keepdims=True)))
    return jnp.einsum('hqk,khd->qhd', probs, values, precision=lax.Precision.HIGHEST)

def layer(state, layer_params, labels):
    gains, shifts, qkv, qv_bias, out_weight, out_bias, up_weight, up_bias, down_weight, down_bias = layer_params
    total_rows = state.shape[0]
    scale = HD ** (-0.5)
    normed = low(norm_rows(state, gains[0], shifts[0]))
    query = low(low_back((dense(normed, qkv[0]) + qv_bias[0]) * scale))
    keys = low(low_back(dense(normed, qkv[1])))
    values = low(low_back(dense(normed, qkv[2]) + qv_bias[1]))
    mixed = attend(query.reshape(total_rows, HEADS, HD), keys.reshape(total_rows, HEADS, HD), values.reshape(total_rows, HEADS, HD), labels).reshape(total_rows, D)
    mixed = low(low_back(mixed))
    middle = state + low_back(dense(mixed, out_weight)) + out_bias
    normed_mid = low(norm_rows(middle, gains[1], shifts[1]))
    hidden = low(jax.nn.gelu(low_back(dense(normed_mid, up_weight) + up_bias), approximate=False))
    return middle + low_back(dense(hidden, down_weight)) + down_bias

def reference(inputs, cotangent, seq_lengths, norm_gain, norm_shift, w_qkv, b_qv, w_out, b_out, w_up, b_up, w_down, b_down):
    params = (norm_gain, norm_shift, w_qkv.astype(jnp.float32), b_qv, w_out.astype(jnp.float32), b_out, w_up.astype(jnp.float32), b_up, w_down.astype(jnp.float32), b_down)
    shards = TOKENS // ROWS
    feed = inputs.astype(jnp.float32).reshape(MICRO * shards, ROWS, D)
    cot_rows = cotangent.astype(jnp.float32).reshape(MICRO * shards, ROWS, D)
    lengths_all = seq_lengths.reshape(MICRO * shards, SLOTS)

    def one_shard(totals, item):
        rows_in, rows_cot, lengths = item
        labels, inside = segments_of(lengths, ROWS)

        def whole(first_in, between, all_params):
            first_params = tuple((member[0] for member in all_params))
            second_params = tuple((member[1] for member in all_params))
            first_out = layer(first_in, first_params, labels)
            second_out = layer(low(low_back(first_out)) + between, second_params, labels)
            return (first_out, second_out)
        zero_rows = jnp.zeros_like(rows_in)
        (first_out, second_out), back = jax.vjp(whole, rows_in, zero_rows, params)
        weighted = rows_cot * inside[:, None].astype(rows_cot.dtype)
        grad_in, grad_between, grad_params = back((jnp.zeros_like(first_out), weighted))
        totals = jax.tree.map(lambda total, term: total + term, totals, grad_params)
        return (totals, (first_out.astype(jnp.bfloat16), second_out.astype(jnp.bfloat16), grad_in.astype(jnp.bfloat16), grad_between.astype(jnp.bfloat16)))
    start_totals = jax.tree.map(jnp.zeros_like, params)
    totals, outs_all = lax.scan(one_shard, start_totals, (feed, cot_rows, lengths_all))
    first_all, second_all, grad_first, grad_second = [member.reshape(MICRO, TOKENS, D) for member in outs_all]
    layer_out = jnp.stack([first_all, second_all])
    input_grad = jnp.stack([grad_first, grad_second])
    return (layer_out, input_grad, totals[0], totals[1], totals[2], totals[3], totals[4], totals[5], totals[6], totals[7], totals[8], totals[9])
```

```python
import functools

import jax
import jax.numpy as jnp
from jax import lax
from jax.experimental import pallas as pl
from jax.experimental.pallas import tpu as pltpu
from jax.sharding import PartitionSpec as P

HD = 64
BF = jnp.bfloat16
F32 = jnp.float32
VMEM = pl.BlockSpec(memory_space=pltpu.VMEM)
SMEM = pl.BlockSpec(memory_space=pltpu.SMEM)
MIB = 1 << 20

GAIN0, GAIN1, SHIFT0, SHIFT1, B_OUT, B_DOWN, B_UP, B_QV = range(8)


def nn(left, right):
    return lax.dot_general(left, right, (((1,), (0,)), ((), ())), preferred_element_type=F32)


def nt(left, right):
    return lax.dot_general(left, right, (((1,), (1,)), ((), ())), preferred_element_type=F32)


def tn(left, right):
    return lax.dot_general(left, right, (((0,), (0,)), ((), ())), preferred_element_type=F32)


def call(body, outs, args, specs=None, scratch=(), flops=0, bytes_accessed=0, vmem=32, name=None):
    return pl.pallas_call(
        body,
        out_shape=[jax.ShapeDtypeStruct(s, d) for s, d in outs],
        in_specs=specs if specs is not None else [VMEM] * len(args),
        out_specs=[VMEM] * len(outs),
        scratch_shapes=list(scratch),
        compiler_params=pltpu.CompilerParams(vmem_limit_bytes=vmem * MIB),
        cost_estimate=pl.CostEstimate(flops=flops, bytes_accessed=bytes_accessed, transcendentals=0),
        name=name,
    )(*args)


def swap(value, axis, by):
    count = lax.axis_size(axis)
    return lax.ppermute(value, axis, [(i, i ^ by) for i in range(count)])


def gather_rel(own):
    return [own] + [swap(own, "tensor", k) for k in range(1, lax.axis_size("tensor"))]


def scatter_rel(parts):
    return [parts[0]] + [swap(parts[k], "tensor", k) for k in range(1, len(parts))]


def row_norm(x):
    mean = jnp.mean(x, axis=-1, keepdims=True)
    centred = x - mean
    var = jnp.mean(centred * centred, axis=-1, keepdims=True)
    inv = lax.rsqrt(var + 1e-05)
    return centred * inv, inv


def norm_back(grad, xhat, inv, gain):
    gx = grad * gain
    m1 = jnp.mean(gx, axis=-1, keepdims=True)
    m2 = jnp.mean(gx * xhat, axis=-1, keepdims=True)
    return inv * (gx - m1 - xhat * m2)


def add_terms(refs):
    total = refs[0][...].astype(F32)
    for ref in refs[1:]:
        total = total + ref[...].astype(F32)
    return total


def first_norm_body(x, vec, out):
    xhat, _ = row_norm(x[...].astype(F32))
    out[...] = (xhat * vec[GAIN0 : GAIN0 + 1, :] + vec[SHIFT0 : SHIFT0 + 1, :]).astype(BF)


def mid_fwd_body(parts, *refs):
    x, vec = refs[:2]
    terms = refs[2 : 2 + parts]
    mid, out = refs[2 + parts :]
    h = x[...].astype(F32) + add_terms(terms) + vec[B_OUT : B_OUT + 1, :]
    mid[...] = h
    xhat, _ = row_norm(h)
    out[...] = (xhat * vec[GAIN1 : GAIN1 + 1, :] + vec[SHIFT1 : SHIFT1 + 1, :]).astype(BF)


def end_fwd_body(parts, *refs):
    mid, vec, vec_next = refs[:3]
    terms = refs[3 : 3 + parts]
    result, out = refs[3 + parts :]
    y = (mid[...] + add_terms(terms) + vec[B_DOWN : B_DOWN + 1, :]).astype(BF)
    result[...] = y
    xhat, _ = row_norm(y.astype(F32))
    out[...] = (xhat * vec_next[GAIN0 : GAIN0 + 1, :] + vec_next[SHIFT0 : SHIFT0 + 1, :]).astype(BF)


def last_fwd_body(parts, *refs):
    mid, vec = refs[:2]
    terms = refs[2 : 2 + parts]
    (result,) = refs[2 + parts :]
    result[...] = (mid[...] + add_terms(terms) + vec[B_DOWN : B_DOWN + 1, :]).astype(BF)


def mid_bwd_body(parts, *refs):
    g, mid, vec = refs[:3]
    terms = refs[3 : 3 + parts]
    grad_mid, grad_low, small = refs[3 + parts :]
    grad = g[...].astype(F32)
    back = add_terms(terms)
    xhat, inv = row_norm(mid[...])
    dh = grad + norm_back(back, xhat, inv, vec[GAIN1 : GAIN1 + 1, :])
    grad_mid[...] = dh
    grad_low[...] = dh.astype(BF)
    small[0:1, :] = jnp.sum(back * xhat, axis=0, keepdims=True)
    small[1:2, :] = jnp.sum(back, axis=0, keepdims=True)
    small[2:3, :] = jnp.sum(dh, axis=0, keepdims=True)
    small[3:4, :] = jnp.sum(grad, axis=0, keepdims=True)


def end_bwd_body(parts, *refs):
    grad_mid, x, vec = refs[:3]
    terms = refs[3 : 3 + parts]
    result, small = refs[3 + parts :]
    back = add_terms(terms)
    xhat, inv = row_norm(x[...].astype(F32))
    result[...] = (grad_mid[...] + norm_back(back, xhat, inv, vec[GAIN0 : GAIN0 + 1, :])).astype(BF)
    small[0:1, :] = jnp.sum(back * xhat, axis=0, keepdims=True)
    small[1:2, :] = jnp.sum(back, axis=0, keepdims=True)


def strip_mask(meta, slots, first, rows, cols):
    place = first + lax.broadcasted_iota(jnp.int32, (rows, 1), 0)
    start = jnp.zeros((rows, 1), jnp.int32)
    for s in range(slots):
        end = meta[1 + s]
        start = jnp.where(place >= end, end, start)
    start = jnp.where(place >= meta[slots], place, start)
    key = lax.broadcasted_iota(jnp.int32, (rows, cols), 1)
    return (key >= start) & (key <= place)


def attend_fwd_body(parts, slots, *refs):
    meta, wqkv, wout, vec = refs[:4]
    pieces = refs[4 : 4 + parts]
    outs = refs[4 + parts : 4 + 2 * parts]
    q, k, v, o, stat = refs[4 + 2 * parts :]
    rank = meta[0]
    block, width = pieces[0].shape[0], wqkv.shape[2]
    qb = vec[B_QV : B_QV + 1, :width]
    vb = vec[B_QV : B_QV + 1, width : 2 * width]
    for j in range(parts):
        rows = pl.ds(pl.multiple_of((rank ^ j) * block, block), block)
        a = pieces[j][...]
        q[rows, :] = ((nn(a, wqkv[0]) + qb) * (HD**-0.5)).astype(BF)
        k[rows, :] = nn(a, wqkv[1]).astype(BF)
        v[rows, :] = (nn(a, wqkv[2]) + vb).astype(BF)
    for i in range(parts):
        rows, cols = slice(i * block, (i + 1) * block), (i + 1) * block
        mask = strip_mask(meta, slots, i * block, block, cols)
        lane = lax.broadcasted_iota(jnp.int32, (block, 128), 1)
        stats = jnp.zeros((block, 128), F32)
        for h in range(width // HD):
            own = slice(h * HD, (h + 1) * HD)
            s = jnp.where(mask, nt(q[rows, own], k[:cols, own]), -1e9)
            top = jnp.max(s, axis=-1, keepdims=True)
            e = jnp.exp(s - top)
            total = jnp.sum(e, axis=-1, keepdims=True)
            p = (e * (1.0 / total)).astype(BF)
            o[rows, own] = nn(p, v[:cols, own]).astype(BF)
            stats = jnp.where(lane == h, top + jnp.log(total), stats)
        stat[rows, :] = stats
    for j in range(parts):
        rows = pl.ds(pl.multiple_of((rank ^ j) * block, block), block)
        outs[j][...] = nt(o[rows, :], wout[...]).astype(BF)


def attend_bwd_body(parts, slots, *refs):
    meta, wqkv, wout, q, k, v, stat = refs[:7]
    pieces = refs[7 : 7 + parts]
    outs = refs[7 + parts : 7 + 2 * parts]
    dq, dk, dv, small, do, dkf, dvf = refs[7 + 2 * parts :]
    rank = meta[0]
    block, width = pieces[0].shape[0], wqkv.shape[2]
    for j in range(parts):
        rows = pl.ds(pl.multiple_of((rank ^ j) * block, block), block)
        do[rows, :] = nn(pieces[j][...], wout[...]).astype(BF)
    for i in reversed(range(parts)):
        rows, cols = slice(i * block, (i + 1) * block), (i + 1) * block
        mask = strip_mask(meta, slots, i * block, block, cols)
        for h in range(width // HD):
            own = slice(h * HD, (h + 1) * HD)
            qh, kh, vh, doh = q[rows, own], k[:cols, own], v[:cols, own], do[rows, own]
            s = jnp.where(mask, nt(qh, kh), -1e9)
            p = jnp.exp(s - stat[rows, h : h + 1])
            dp = nt(doh, vh)
            inner = jnp.sum(dp * p, axis=-1, keepdims=True)
            ds = (p * (dp - inner)).astype(BF)
            dq[rows, own] = (nn(ds, kh).astype(BF).astype(F32) * (HD**-0.5)).astype(BF)
            dkh, dvh = tn(ds, qh), tn(p.astype(BF), doh)
            if i == parts - 1:
                dkf[h] = dkh
                dvf[h] = dvh
            else:
                dkf[h, :cols] += dkh
                dvf[h, :cols] += dvh
    for h in range(width // HD):
        own = slice(h * HD, (h + 1) * HD)
        dk[:, own] = dkf[h].astype(BF)
        dv[:, own] = dvf[h].astype(BF)
    small[0:1, :] = jnp.sum(dq[...].astype(F32), axis=0, keepdims=True)
    small[1:2, :] = jnp.sum(dv[...].astype(F32), axis=0, keepdims=True)
    for j in range(parts):
        rows = pl.ds(pl.multiple_of((rank ^ j) * block, block), block)
        outs[j][...] = (
            nt(dq[rows, :], wqkv[0]) + nt(dk[rows, :], wqkv[1]) + nt(dv[rows, :], wqkv[2])
        ).astype(BF)


def attend_weights_body(parts, *refs):
    meta, o, dq, dk, dv = refs[:5]
    normed = refs[5 : 5 + parts]
    grads = refs[5 + parts : 5 + 2 * parts]
    gqkv, gout = refs[5 + 2 * parts :]
    rank = meta[0]
    block = normed[0].shape[0]
    totals = [None] * 4
    for j in range(parts):
        rows = pl.ds(pl.multiple_of((rank ^ j) * block, block), block)
        a, g = normed[j][...], grads[j][...]
        terms = [tn(a, dq[rows, :]), tn(a, dk[rows, :]), tn(a, dv[rows, :]), tn(g, o[rows, :])]
        totals = [t if s is None else s + t for s, t in zip(totals, terms)]
    for n in range(3):
        gqkv[n] = totals[n].astype(BF)
    gout[...] = totals[3].astype(BF)


def feed_fwd_body(parts, *refs):
    wup, wdown, vec = refs[:3]
    pieces = refs[3 : 3 + parts]
    outs = refs[3 + parts : 3 + 2 * parts]
    hidden, slope = refs[3 + 2 * parts :]
    block = pieces[0].shape[0]
    bias = vec[B_UP : B_UP + 1, : wup.shape[1]]
    for j in range(parts):
        rows = slice(j * block, (j + 1) * block)
        u = nn(pieces[j][...], wup[...]) + bias
        share = 0.5 * (1.0 + lax.erf(u * (0.5**0.5)))
        f = (u * share).astype(BF)
        hidden[rows, :] = f
        slope[rows, :] = share + u * (jnp.exp(-0.5 * (u * u)) * 0.3989422804014327)
        outs[j][...] = nt(f, wdown[...]).astype(BF)


def feed_bwd_body(parts, *refs):
    wup, wdown, slope = refs[:3]
    pieces = refs[3 : 3 + parts]
    outs = refs[3 + parts : 3 + 2 * parts]
    du, small = refs[3 + 2 * parts :]
    block = pieces[0].shape[0]
    total = None
    for j in range(parts):
        rows = slice(j * block, (j + 1) * block)
        d = (nn(pieces[j][...], wdown[...]) * slope[rows, :]).astype(BF)
        du[rows, :] = d
        term = jnp.sum(d.astype(F32), axis=0, keepdims=True)
        total = term if total is None else total + term
        outs[j][...] = nt(d, wup[...]).astype(BF)
    small[...] = total


def feed_weights_body(parts, *refs):
    hidden, du = refs[:2]
    normed = refs[2 : 2 + parts]
    grads = refs[2 + parts : 2 + 2 * parts]
    gup, gdown = refs[2 + 2 * parts :]
    block = normed[0].shape[0]
    up = down = None
    for j in range(parts):
        rows = slice(j * block, (j + 1) * block)
        t_up, t_down = tn(normed[j][...], du[rows, :]), tn(grads[j][...], hidden[rows, :])
        up, down = (t_up, t_down) if up is None else (up + t_up, down + t_down)
    gup[...] = up.astype(BF)
    gdown[...] = down.astype(BF)


def gather_dp(shard, dim):
    count = lax.axis_size("dp")
    if count > 8:
        return lax.all_gather(shard, "dp", axis=dim, tiled=True)
    rank = lax.axis_index("dp")
    size = shard.shape[dim]
    whole = jnp.zeros(shard.shape[:dim] + (size * count,) + shard.shape[dim + 1 :], shard.dtype)
    for k in range(count):
        piece = shard if k == 0 else swap(shard, "dp", k)
        whole = lax.dynamic_update_slice_in_dim(whole, piece, (rank ^ k) * size, dim)
    return whole


def sum_to_owner(grad, layer, dim):
    count = lax.axis_size("dp")
    grad = grad.astype(F32) + lax.ppermute(grad, "section", [(1 - layer, layer)]).astype(F32)
    grad = grad.astype(BF)
    if count > 8:
        return lax.psum_scatter(grad, "dp", scatter_dimension=dim, tiled=True).astype(F32)
    rank = lax.axis_index("dp")
    size = grad.shape[dim] // count
    total = lax.dynamic_slice_in_dim(grad, rank * size, size, dim).astype(F32)
    for k in range(1, count):
        block = lax.dynamic_slice_in_dim(grad, (rank ^ k) * size, size, dim)
        pairs = [(layer * count + i, layer * count + (i ^ k)) for i in range(count)]
        total = total + lax.ppermute(block, ("section", "dp"), pairs).astype(F32)
    return total


def sum_small(value, axis):
    count = lax.axis_size(axis)
    if count > 8:
        return lax.psum(value, axis)
    total = value
    for k in range(1, count):
        total = total + swap(value, axis, k)
    return total


def shards(
    inputs,
    cotangent,
    seq_lengths,
    norm_gain,
    norm_shift,
    w_qkv,
    b_qv,
    w_out,
    b_out,
    w_up,
    b_up,
    w_down,
    b_down,
):
    section = lax.axis_index("section")
    rank = lax.axis_index("tensor")
    parts = lax.axis_size("tensor")
    own_first = section == 0
    rows, width = inputs.shape[1], inputs.shape[2]
    total_rows = rows * parts
    slots = seq_lengths.shape[2]
    heads = w_qkv.shape[3]
    units = w_up.shape[2]

    def by_layer(own, other):
        return jnp.where(own_first, own, other), jnp.where(own_first, other, own)

    def both_layers(own):
        return by_layer(own, swap(own, "section", 1))

    def pad(row):
        return jnp.pad(row.reshape(1, -1), ((0, 0), (0, width - row.size)))

    packed = jnp.concatenate(
        [norm_gain[0], norm_shift[0], b_out, b_down, pad(b_up[0]), pad(b_qv[0])], axis=0
    )
    vec = both_layers(packed)
    x0 = lax.dynamic_index_in_dim(inputs, section, 0, keepdims=False)
    (normed,) = call(first_norm_body, [((rows, width), BF)], [x0, vec[0]], name="norm_first")
    a0 = gather_rel(normed)
    wqkv = both_layers(gather_dp(w_qkv[0], 1))
    wout = both_layers(gather_dp(w_out[0].T, 0))
    wup = both_layers(gather_dp(w_up[0], 0))
    wdown = both_layers(gather_dp(w_down[0].T, 0))

    lengths = lax.dynamic_index_in_dim(seq_lengths[:, 0], section, 0, keepdims=False)
    ends = jnp.cumsum(lengths).astype(jnp.int32)
    meta = jnp.concatenate([rank.astype(jnp.int32)[None], ends])
    place = rank * rows + jnp.arange(rows, dtype=jnp.int32)
    valid = (place < ends[-1])[:, None]
    cot = lax.dynamic_index_in_dim(cotangent, section, 0, keepdims=False)
    grad1 = jnp.where(valid, cot, jnp.zeros_like(cot))
    block_out = [((rows, width), BF)] * parts
    tall = ((total_rows, heads), BF)

    def attend_fwd(layer, pieces):
        res = call(
            functools.partial(attend_fwd_body, parts, slots),
            block_out + [tall, tall, tall, tall, ((total_rows, 128), F32)],
            [meta, wqkv[layer], wout[layer], vec[layer], *pieces],
            specs=[SMEM] + [VMEM] * (3 + parts),
            flops=4 * 10**9,
            bytes_accessed=8 * 10**6,
            vmem=40,
            name="attend_fwd",
        )
        return res[:parts], res[parts:]

    def feed_fwd(layer, pieces):
        res = call(
            functools.partial(feed_fwd_body, parts),
            block_out + [((total_rows, units), BF), ((total_rows, units), F32)],
            [wup[layer], wdown[layer], vec[layer], *pieces],
            flops=4 * 10**9,
            bytes_accessed=12 * 10**6,
            vmem=40,
            name="feed_fwd",
        )
        return res[:parts], res[parts:]

    def mid_fwd(layer, x, terms):
        return call(
            functools.partial(mid_fwd_body, parts),
            [((rows, width), F32), ((rows, width), BF)],
            [x, vec[layer], *terms],
            name="mid_fwd",
        )

    out0, att0 = attend_fwd(0, a0)
    mid0, normed = mid_fwd(0, x0, scatter_rel(out0))
    c0 = gather_rel(normed)
    down0, feed0 = feed_fwd(0, c0)
    x1, normed = call(
        functools.partial(end_fwd_body, parts),
        [((rows, width), BF), ((rows, width), BF)],
        [mid0, vec[0], vec[1], *scatter_rel(down0)],
        name="end_fwd",
    )
    a1 = gather_rel(normed)
    out1, att1 = attend_fwd(1, a1)
    mid1, normed = mid_fwd(1, x1, scatter_rel(out1))
    c1 = gather_rel(normed)
    g1 = gather_rel(grad1)
    down1, feed1 = feed_fwd(1, c1)
    (x2,) = call(
        functools.partial(last_fwd_body, parts),
        [((rows, width), BF)],
        [mid1, vec[1], *scatter_rel(down1)],
        name="last_fwd",
    )

    def layer_back(layer, grad, g, x, a, att, mid, c, feed):
        q, k, v, o, stat = att
        hidden, slope = feed
        res = call(
            functools.partial(feed_bwd_body, parts),
            block_out + [((total_rows, units), BF), ((1, units), F32)],
            [wup[layer], wdown[layer], slope, *g],
            flops=3 * 10**9,
            bytes_accessed=12 * 10**6,
            vmem=40,
            name="feed_bwd",
        )
        terms, (du, small_up) = scatter_rel(res[:parts]), res[parts:]
        gup, gdown = call(
            functools.partial(feed_weights_body, parts),
            [((width, units), BF), ((width, units), BF)],
            [hidden, du, *c, *g],
            flops=3 * 10**9,
            bytes_accessed=10 * 10**6,
            vmem=40,
            name="feed_weights",
        )
        dmid, dlow, small_mid = call(
            functools.partial(mid_bwd_body, parts),
            [((rows, width), F32), ((rows, width), BF), ((4, width), F32)],
            [grad, mid, vec[layer], *terms],
            name="mid_bwd",
        )
        hb = gather_rel(dlow)
        res = call(
            functools.partial(attend_bwd_body, parts, slots),
            block_out + [tall, tall, tall, ((2, heads), F32)],
            [meta, wqkv[layer], wout[layer], q, k, v, stat, *hb],
            specs=[SMEM] + [VMEM] * (6 + parts),
            scratch=[
                pltpu.VMEM((total_rows, heads), BF),
                pltpu.VMEM((heads // HD, total_rows, HD), F32),
                pltpu.VMEM((heads // HD, total_rows, HD), F32),
            ],
            flops=8 * 10**9,
            bytes_accessed=8 * 10**6,
            vmem=40,
            name="attend_bwd",
        )
        terms, (dq, dk, dv, small_qv) = scatter_rel(res[:parts]), res[parts:]
        gqkv, gout = call(
            functools.partial(attend_weights_body, parts),
            [((3, width, heads), BF), ((width, heads), BF)],
            [meta, o, dq, dk, dv, *a, *hb],
            specs=[SMEM] + [VMEM] * (4 + 2 * parts),
            flops=2 * 10**9,
            bytes_accessed=6 * 10**6,
            vmem=40,
            name="attend_weights",
        )
        dx, small_end = call(
            functools.partial(end_bwd_body, parts),
            [((rows, width), BF), ((2, width), F32)],
            [dmid, x, vec[layer], *terms],
            name="end_bwd",
        )
        totals = (
            sum_to_owner(gdown, layer, 0),
            sum_to_owner(gup, layer, 0),
            sum_to_owner(gout, layer, 0),
            sum_to_owner(gqkv, layer, 1),
        )
        return dx, totals, (small_end, small_mid, small_up, small_qv)

    dx1, totals1, small1 = layer_back(1, grad1, g1, x1, a1, att1, mid1, c1, feed1)
    g0 = gather_rel(dx1)
    dx0, totals0, small0 = layer_back(0, dx1, g0, x0, a0, att0, mid0, c0, feed0)

    gdown, gup, gout, gqkv = [
        jnp.where(own_first, first, second) for first, second in zip(totals0, totals1)
    ]

    def collect(first, second):
        keep = jnp.where(own_first, first, second)
        came = swap(jnp.where(own_first, second, first), "section", 1)
        low, high = by_layer(keep, came)
        return jnp.stack([low, high])[None]

    layer_out = collect(x1, x2)
    input_grad = collect(dx0, dx1)

    def pack_small(small):
        end, mid, up, qv = small
        return jnp.concatenate([end, mid], axis=0), jnp.concatenate([pad(up), pad(qv)], axis=0)

    whole0, part0 = pack_small(small0)
    whole1, part1 = pack_small(small1)
    whole = sum_small(jnp.where(own_first, whole0, whole1), "tensor")
    whole_away = sum_small(jnp.where(own_first, whole1, whole0), "tensor")
    mine = jnp.concatenate([whole, jnp.where(own_first, part0, part1)], axis=0)
    away = jnp.concatenate([whole_away, jnp.where(own_first, part1, part0)], axis=0)
    mine = sum_small(mine + swap(away, "section", 1), "dp")
    return (
        layer_out,
        input_grad,
        jnp.stack([mine[0], mine[2]])[None],
        jnp.stack([mine[1], mine[3]])[None],
        gqkv[None],
        mine[7, : 2 * heads].reshape(1, 2, heads),
        gout.T[None],
        mine[4][None],
        gup[None],
        mine[6, :units][None],
        gdown.T[None],
        mine[5][None],
    )


def solution(mesh):
    in_specs = (
        P(None, ("dp", "tensor"), None),
        P(None, ("dp", "tensor"), None),
        P(None, "dp", None),
        P("section", None, None),
        P("section", None, None),
        P("section", None, "dp", "tensor"),
        P("section", None, "tensor"),
        P("section", "tensor", "dp"),
        P("section", None),
        P("section", "dp", "tensor"),
        P("section", "tensor"),
        P("section", "tensor", "dp"),
        P("section", None),
    )
    out_specs = (
        P("section", None, ("dp", "tensor"), None),
        P("section", None, ("dp", "tensor"), None),
        P("section", None, None),
        P("section", None, None),
        P("section", None, "dp", "tensor"),
        P("section", None, "tensor"),
        P("section", "tensor", "dp"),
        P("section", None),
        P("section", "dp", "tensor"),
        P("section", "tensor"),
        P("section", "tensor", "dp"),
        P("section", None),
    )
    return jax.shard_map(shards, mesh=mesh, in_specs=in_specs, out_specs=out_specs, check_vma=False)
```

```python
import functools

import jax
import jax.numpy as jnp
from jax import lax
from jax.experimental import pallas as pl
from jax.experimental.pallas import tpu as pltpu
from jax.sharding import PartitionSpec as P

HD = 64
BF = jnp.bfloat16
F32 = jnp.float32
VMEM = pl.BlockSpec(memory_space=pltpu.VMEM)
SMEM = pl.BlockSpec(memory_space=pltpu.SMEM)
MIB = 1 << 20

RANK, MICRO, DP, LAST, HALF, META = range(6)

GAIN0, GAIN1, SHIFT0, SHIFT1, B_OUT, B_DOWN, B_UP, B_QV = range(8)


def nn(left, right):
    return lax.dot_general(left, right, (((1,), (0,)), ((), ())), preferred_element_type=F32)


def nt(left, right):
    return lax.dot_general(left, right, (((1,), (1,)), ((), ())), preferred_element_type=F32)


def tn(left, right):
    return lax.dot_general(left, right, (((0,), (0,)), ((), ())), preferred_element_type=F32)


def call(
    body, outs, args, scalars=None, tokens=(), scratch=(), vmem=16, name=None
):
    args = ([] if scalars is None else [scalars]) + list(args)
    count = len(args)

    def kernel(*refs):
        body(*refs[:count], *refs[count + len(tokens) :])

    return pl.pallas_call(
        kernel,
        out_shape=[jax.ShapeDtypeStruct(s, d) for s, d in outs],
        in_specs=([] if scalars is None else [SMEM])
        + [VMEM] * (count - (scalars is not None))
        + [pl.BlockSpec(memory_space=pl.ANY)] * len(tokens),
        out_specs=[VMEM] * len(outs),
        scratch_shapes=list(scratch),
        compiler_params=pltpu.CompilerParams(vmem_limit_bytes=vmem * MIB),
        cost_estimate=pl.CostEstimate(flops=1, bytes_accessed=1, transcendentals=0),
        name=name,
    )(*args, *tokens)


def swap(value, axis, by):
    count = lax.axis_size(axis)
    return lax.ppermute(value, axis, [(i, i ^ by) for i in range(count)])


def seat(micro, rank):
    half = lax.axis_size("tensor") // 2
    return rank // half * 2 * half + micro * half + rank % half


def permute(value, pairs):
    return lax.ppermute(value, ("section", "tensor"), pairs)


def seats():
    return [(m, r) for m in range(2) for r in range(lax.axis_size("tensor"))]


def swap_micro(value):
    return permute(value, [(seat(m, r), seat(1 - m, r)) for m, r in seats()])


def swap_rank(value, by):
    return permute(value, [(seat(m, r), seat(m, r ^ by)) for m, r in seats()])


def take_seat(value, flip):
    count = lax.axis_size("tensor")
    return permute(value, [((m ^ flip) * count + r, seat(m, r)) for m, r in seats()])


def leave_seat(value, flip):
    count = lax.axis_size("tensor")
    return permute(value, [(seat(m, r), (m ^ flip) * count + r) for m, r in seats()])


def gather_rel(own):
    chip = swap_rank(own, 1)
    return [own, chip, swap_rank(own, 2), swap_rank(chip, 2)]


def scatter_rel(parts):
    far = swap_rank(parts[3], 2)
    near = swap_rank(parts[2], 2)
    chip = (parts[1].astype(F32) + far.astype(F32)).astype(BF)
    return [parts[0], near, swap_rank(chip, 1)]


def row_norm(x):
    mean = jnp.mean(x, axis=-1, keepdims=True)
    centred = x - mean
    var = jnp.mean(centred * centred, axis=-1, keepdims=True)
    inv = lax.rsqrt(var + 1e-05)
    return centred * inv, inv


def norm_back(grad, xhat, inv, gain):
    gx = grad * gain
    m1 = jnp.mean(gx, axis=-1, keepdims=True)
    m2 = jnp.mean(gx * xhat, axis=-1, keepdims=True)
    return inv * (gx - m1 - xhat * m2)


def add_terms(refs):
    total = refs[0][...].astype(F32)
    for ref in refs[1:]:
        total = total + ref[...].astype(F32)
    return total


def first_norm_body(x, vec, out):
    xhat, _ = row_norm(x[...].astype(F32))
    out[...] = (xhat * vec[GAIN0 : GAIN0 + 1, :] + vec[SHIFT0 : SHIFT0 + 1, :]).astype(BF)


def mid_fwd_body(parts, *refs):
    x, vec = refs[:2]
    terms = refs[2 : 2 + parts]
    mid, out = refs[2 + parts :]
    h = x[...].astype(F32) + add_terms(terms) + vec[B_OUT : B_OUT + 1, :]
    mid[...] = h
    xhat, _ = row_norm(h)
    out[...] = (xhat * vec[GAIN1 : GAIN1 + 1, :] + vec[SHIFT1 : SHIFT1 + 1, :]).astype(BF)


def end_fwd_body(parts, *refs):
    mid, vec, vec_next = refs[:3]
    terms = refs[3 : 3 + parts]
    result, out = refs[3 + parts :]
    y = (mid[...] + add_terms(terms) + vec[B_DOWN : B_DOWN + 1, :]).astype(BF)
    result[...] = y
    xhat, _ = row_norm(y.astype(F32))
    out[...] = (xhat * vec_next[GAIN0 : GAIN0 + 1, :] + vec_next[SHIFT0 : SHIFT0 + 1, :]).astype(BF)


def last_fwd_body(parts, *refs):
    mid, vec = refs[:2]
    terms = refs[2 : 2 + parts]
    (result,) = refs[2 + parts :]
    result[...] = (mid[...] + add_terms(terms) + vec[B_DOWN : B_DOWN + 1, :]).astype(BF)


def mid_bwd_body(parts, *refs):
    g, mid, vec = refs[:3]
    terms = refs[3 : 3 + parts]
    grad_mid, grad_low, small = refs[3 + parts :]
    grad = g[...].astype(F32)
    back = add_terms(terms)
    xhat, inv = row_norm(mid[...])
    dh = grad + norm_back(back, xhat, inv, vec[GAIN1 : GAIN1 + 1, :])
    grad_mid[...] = dh
    grad_low[...] = dh.astype(BF)
    small[0:1, :] = jnp.sum(back * xhat, axis=0, keepdims=True)
    small[1:2, :] = jnp.sum(back, axis=0, keepdims=True)
    small[2:3, :] = jnp.sum(dh, axis=0, keepdims=True)
    small[3:4, :] = jnp.sum(grad, axis=0, keepdims=True)


def end_bwd_body(parts, *refs):
    grad_mid, x, vec = refs[:3]
    terms = refs[3 : 3 + parts]
    result, small = refs[3 + parts :]
    back = add_terms(terms)
    xhat, inv = row_norm(x[...].astype(F32))
    result[...] = (grad_mid[...] + norm_back(back, xhat, inv, vec[GAIN0 : GAIN0 + 1, :])).astype(BF)
    small[0:1, :] = jnp.sum(back * xhat, axis=0, keepdims=True)
    small[1:2, :] = jnp.sum(back, axis=0, keepdims=True)


def chosen(flag, first, second):
    return jnp.where(flag == 0, first[...], second[...])


def ordered_rows(rank, by, block):
    return pl.ds(pl.multiple_of((rank ^ by) * block, 8), block)


def strip_mask(meta, slots, first, rows, cols):
    place = first + lax.broadcasted_iota(jnp.int32, (rows, 1), 0)
    start = jnp.zeros((rows, 1), jnp.int32)
    for s in range(slots):
        end = meta[META + s]
        start = jnp.where(place >= end, end, start)
    start = jnp.where(place >= meta[META + slots - 1], place, start)
    key = lax.broadcasted_iota(jnp.int32, (rows, cols), 1)
    return (key >= start) & (key <= place)


def attend_fwd_body(parts, slots, *refs):
    meta, own_w, other_w, vec = refs[:4]
    pieces = refs[4 : 4 + parts]
    outs = refs[4 + parts : 4 + 2 * parts]
    q, k, v, o, stat = refs[4 + 2 * parts :]
    rank = meta[RANK]
    block, width = pieces[0].shape[0], own_w.shape[1] // 2
    wqk = chosen(meta[MICRO], own_w, other_w)
    wvo = chosen(meta[MICRO], other_w, own_w)
    wq, wk, wv, wout = wqk[:, :width], wqk[:, width:], wvo[:, :width], wvo[:, width:]
    qb = vec[B_QV : B_QV + 1, :width]
    vb = vec[B_QV : B_QV + 1, width : 2 * width]
    for j in range(parts):
        rows = ordered_rows(rank, j, block)
        a = pieces[j][...]
        q[rows, :] = ((nn(a, wq) + qb) * (HD**-0.5)).astype(BF)
        k[rows, :] = nn(a, wk).astype(BF)
        v[rows, :] = (nn(a, wv) + vb).astype(BF)
    for i in range(parts):
        rows, cols = slice(i * block, (i + 1) * block), (i + 1) * block
        mask = strip_mask(meta, slots, i * block, block, cols)
        lane = lax.broadcasted_iota(jnp.int32, (block, 128), 1)
        stats = jnp.zeros((block, 128), F32)
        for h in range(width // HD):
            own = slice(h * HD, (h + 1) * HD)
            s = jnp.where(mask, nt(q[rows, own], k[:cols, own]), -1e9)
            top = jnp.max(s, axis=-1, keepdims=True)
            e = jnp.exp(s - top)
            total = jnp.sum(e, axis=-1, keepdims=True)
            p = (e * (1.0 / total)).astype(BF)
            o[rows, own] = nn(p, v[:cols, own]).astype(BF)
            stats = jnp.where(lane == h, top + jnp.log(total), stats)
        stat[rows, :] = stats
    for j in range(parts):
        outs[j][...] = nt(o[ordered_rows(rank, j, block), :], wout).astype(BF)


def attend_bwd_body(parts, slots, *refs):
    meta, own_w, other_w, q, k, v, stat = refs[:7]
    pieces = refs[7 : 7 + parts]
    outs = refs[7 + parts : 7 + 2 * parts]
    dq, dk, dv, small, do, dkf, dvf = refs[7 + 2 * parts :]
    rank = meta[RANK]
    block, width = pieces[0].shape[0], own_w.shape[1] // 2
    wqk = chosen(meta[MICRO], own_w, other_w)
    wvo = chosen(meta[MICRO], other_w, own_w)
    wq, wk, wv, wout = wqk[:, :width], wqk[:, width:], wvo[:, :width], wvo[:, width:]
    for j in range(parts):
        do[ordered_rows(rank, j, block), :] = nn(pieces[j][...], wout).astype(BF)
    for i in reversed(range(parts)):
        rows, cols = slice(i * block, (i + 1) * block), (i + 1) * block
        mask = strip_mask(meta, slots, i * block, block, cols)
        for h in range(width // HD):
            own = slice(h * HD, (h + 1) * HD)
            qh, kh, vh, doh = q[rows, own], k[:cols, own], v[:cols, own], do[rows, own]
            s = jnp.where(mask, nt(qh, kh), -1e9)
            p = jnp.exp(s - stat[rows, h : h + 1])
            dp = nt(doh, vh)
            inner = jnp.sum(dp * p, axis=-1, keepdims=True)
            ds = (p * (dp - inner)).astype(BF)
            dq[rows, own] = (nn(ds, kh).astype(BF).astype(F32) * (HD**-0.5)).astype(BF)
            dkh, dvh = tn(ds, qh), tn(p.astype(BF), doh)
            if i == parts - 1:
                dkf[h] = dkh
                dvf[h] = dvh
            else:
                dkf[h, :cols] += dkh
                dvf[h, :cols] += dvh
    for h in range(width // HD):
        own = slice(h * HD, (h + 1) * HD)
        dk[:, own] = dkf[h].astype(BF)
        dv[:, own] = dvf[h].astype(BF)
    small[0:1, :] = jnp.sum(dq[...].astype(F32), axis=0, keepdims=True)
    small[1:2, :] = jnp.sum(dv[...].astype(F32), axis=0, keepdims=True)
    for j in range(parts):
        rows = ordered_rows(rank, j, block)
        outs[j][...] = (nt(dq[rows, :], wq) + nt(dk[rows, :], wk) + nt(dv[rows, :], wv)).astype(BF)


def attend_weights_body(parts, *refs):
    meta, o, dq, dk, dv = refs[:5]
    normed = refs[5 : 5 + parts]
    grads = refs[5 + parts : 5 + 2 * parts]
    keep, send = refs[5 + 2 * parts :]
    rank, flag = meta[RANK], meta[MICRO]
    block, width = normed[0].shape[0], o.shape[1]
    totals = [None] * 4
    for j in range(parts):
        rows = ordered_rows(rank, j, block)
        a, g = normed[j][...], grads[j][...]
        terms = [tn(a, dq[rows, :]), tn(a, dk[rows, :]), tn(a, dv[rows, :]), tn(g, o[rows, :])]
        totals = [t if s is None else s + t for s, t in zip(totals, terms)]
    q, k, v, out = [t.astype(BF) for t in totals]
    keep[:, :width] = jnp.where(flag == 0, q, v)
    keep[:, width:] = jnp.where(flag == 0, k, out)
    send[:, :width] = jnp.where(flag == 0, v, q)
    send[:, width:] = jnp.where(flag == 0, out, k)


def feed_fwd_body(parts, *refs):
    meta, own_w, other_w, vec = refs[:4]
    pieces = refs[4 : 4 + parts]
    outs = refs[4 + parts : 4 + 2 * parts]
    hidden, slope = refs[4 + 2 * parts :]
    block = pieces[0].shape[0]
    wup = chosen(meta[MICRO], own_w, other_w)
    wdown = chosen(meta[MICRO], other_w, own_w)
    bias = vec[B_UP : B_UP + 1, : wup.shape[1]]
    for j in range(parts):
        rows = slice(j * block, (j + 1) * block)
        u = nn(pieces[j][...], wup) + bias
        share = 0.5 * (1.0 + lax.erf(u * (0.5**0.5)))
        f = (u * share).astype(BF)
        hidden[rows, :] = f
        slope[rows, :] = share + u * (jnp.exp(-0.5 * (u * u)) * 0.3989422804014327)
        outs[j][...] = nt(f, wdown).astype(BF)


def feed_bwd_body(parts, *refs):
    meta, own_w, other_w, slope = refs[:4]
    pieces = refs[4 : 4 + parts]
    outs = refs[4 + parts : 4 + 2 * parts]
    du, small = refs[4 + 2 * parts :]
    block = pieces[0].shape[0]
    wup = chosen(meta[MICRO], own_w, other_w)
    wdown = chosen(meta[MICRO], other_w, own_w)
    total = None
    for j in range(parts):
        rows = slice(j * block, (j + 1) * block)
        d = (nn(pieces[j][...], wdown) * slope[rows, :]).astype(BF)
        du[rows, :] = d
        term = jnp.sum(d.astype(F32), axis=0, keepdims=True)
        total = term if total is None else total + term
        outs[j][...] = nt(d, wup).astype(BF)
    small[...] = total


def feed_weights_body(parts, *refs):
    meta, hidden, du = refs[:3]
    normed = refs[3 : 3 + parts]
    grads = refs[3 + parts : 3 + 2 * parts]
    keep, send = refs[3 + 2 * parts :]
    flag = meta[MICRO]
    block = normed[0].shape[0]
    up = down = None
    for j in range(parts):
        rows = slice(j * block, (j + 1) * block)
        t_up, t_down = tn(normed[j][...], du[rows, :]), tn(grads[j][...], hidden[rows, :])
        up, down = (t_up, t_down) if up is None else (up + t_up, down + t_down)
    up, down = up.astype(BF), down.astype(BF)
    keep[...] = jnp.where(flag == 0, up, down)
    send[...] = jnp.where(flag == 0, down, up)


def layer_slice_body(layer, meta, own, other, out):
    out[...] = chosen(meta[MICRO] ^ layer, own, other)


def masked_body(meta, x, out):
    rows = x.shape[0]
    place = meta[RANK] * rows + lax.broadcasted_iota(jnp.int32, (rows, 1), 0)
    out[...] = jnp.where(place < meta[LAST], x[...].astype(F32), 0.0).astype(BF)


def assemble_body(meta, *refs):
    pieces, out = refs[:-1], refs[-1]
    size = pieces[0].shape[0]
    for k, piece in enumerate(pieces):
        out[ordered_rows(meta[DP], k, size), :] = piece[...]


def pair_sum_body(meta, keep, came, *outs):
    size = outs[0].shape[0]
    for k, out in enumerate(outs):
        rows = ordered_rows(meta[DP], k, size)
        out[...] = (keep[rows, :].astype(F32) + came[rows, :].astype(F32)).astype(out.dtype)


def collect_body(meta, own, other, out):
    flag = jnp.where(meta[RANK] < meta[HALF], 0, 1)
    out[0] = chosen(flag, own, other)
    out[1] = chosen(flag, other, own)


def total_body(*refs):
    refs[-1][...] = add_terms(refs[:-1]).astype(refs[-1].dtype)


def gather_dp(shard, meta, tokens=()):
    count = lax.axis_size("dp")
    if count > 8:
        return lax.all_gather(shard, "dp", axis=0, tiled=True)
    pieces = [shard] + [swap(shard, "dp", k) for k in range(1, count)]
    shape = (shard.shape[0] * count, shard.shape[1])
    (whole,) = call(assemble_body, [(shape, BF)], pieces, scalars=meta, tokens=tokens, name="assemble")
    return whole


def pair_sum(keep, came, meta, tokens=()):
    count = lax.axis_size("dp")
    if count > 8:
        return [(keep.astype(F32) + came.astype(F32)).astype(BF)]
    shape = (keep.shape[0] // count, keep.shape[1])
    return call(
        pair_sum_body,
        [(shape, F32)] + [(shape, BF)] * (count - 1),
        [keep, came],
        scalars=meta,
        tokens=tokens,
        name="pair_sum",
    )


def sum_blocks(blocks, tokens=()):
    if len(blocks) == 1:
        return lax.psum_scatter(blocks[0], "dp", scatter_dimension=0, tiled=True)
    terms = [blocks[0]] + [swap(blocks[k], "dp", k) for k in range(1, len(blocks))]
    (total,) = call(total_body, [(blocks[0].shape, BF)], terms, tokens=tokens, name="total")
    return total


def sum_dp(value, tokens=()):
    count = lax.axis_size("dp")
    if count > 8:
        return lax.psum(value, "dp")
    terms = [value] + [swap(value, "dp", k) for k in range(1, count)]
    (total,) = call(total_body, [(value.shape, F32)], terms, tokens=tokens, name="sum_dp")
    return total


def sum_ranks(value, tokens=()):
    terms = [value] + [swap_rank(value, k) for k in range(1, lax.axis_size("tensor"))]
    (total,) = call(total_body, [(value.shape, F32)], terms, tokens=tokens, name="sum_ranks")
    return total


def shards(
    inputs,
    cotangent,
    seq_lengths,
    norm_gain,
    norm_shift,
    w_qkv,
    b_qv,
    w_out,
    b_out,
    w_up,
    b_up,
    w_down,
    b_down,
):
    parts = lax.axis_size("tensor")
    section, place = lax.axis_index("section"), lax.axis_index("tensor")
    micro = place // (parts // 2)
    rank = section * (parts // 2) + place % (parts // 2)
    own_first = micro == 0
    rows, width = inputs.shape[1], inputs.shape[2]
    total_rows = rows * parts
    slots = seq_lengths.shape[2]
    heads = w_qkv.shape[3]
    units = w_up.shape[2]

    def by_layer(own, other):
        return jnp.where(own_first, own, other), jnp.where(own_first, other, own)

    def pad(row):
        return jnp.pad(row.reshape(1, -1), ((0, 0), (0, width - row.size)))

    lengths = lax.dynamic_index_in_dim(seq_lengths[:, 0], micro, 0, keepdims=False)
    ends = jnp.cumsum(lengths).astype(jnp.int32)
    meta = [rank, micro, lax.axis_index("dp"), ends[-1], parts // 2]
    meta = jnp.stack([jnp.asarray(m, jnp.int32) for m in meta])
    meta = jnp.concatenate([meta, ends])
    block_out = [((rows, width), BF)] * parts
    tall = ((total_rows, heads), BF)

    def slices_of(first, second):
        own = take_seat(jnp.where(section == 0, first, second), 0)
        other = take_seat(jnp.where(section == 0, second, first), 1)
        return own, other

    def layer_slice(slices, layer, tokens=()):
        (out,) = call(
            functools.partial(layer_slice_body, layer),
            [(slices[0].shape, BF)],
            slices,
            scalars=meta,
            tokens=tokens,
            name="layer_slice",
        )
        return out

    def whole_pair(slices, tokens=()):
        own = gather_dp(slices, meta, tokens)
        return own, swap_micro(own)

    packed = jnp.concatenate(
        [norm_gain[0], norm_shift[0], b_out, b_down, pad(b_up[0]), pad(b_qv[0])], axis=0
    )
    x0 = take_seat(lax.dynamic_index_in_dim(inputs, section, 0, keepdims=False), 0)
    vec = by_layer(take_seat(packed, 0), take_seat(packed, 1))
    attend_first = jnp.concatenate([w_qkv[0, 0], w_qkv[0, 1]], axis=1)
    attend_second = jnp.concatenate([w_qkv[0, 2], w_out[0].T], axis=1)
    attend_slices = slices_of(attend_first, attend_second)
    feed_slices = slices_of(w_up[0], w_down[0].T)
    wattend0 = whole_pair(layer_slice(attend_slices, 0), feed_slices)
    (normed,) = call(first_norm_body, [((rows, width), BF)], [x0, vec[0]], name="norm_first")
    a0 = gather_rel(normed)
    feed_slice0 = layer_slice(feed_slices, 0, [wattend0[0]])

    def attend_fwd(layer, pieces, weights, tokens=()):
        res = call(
            functools.partial(attend_fwd_body, parts, slots),
            block_out + [tall, tall, tall, tall, ((total_rows, 128), F32)],
            [*weights, vec[layer], *pieces],
            scalars=meta,
            vmem=24,
            tokens=tokens,
            name="attend_fwd",
        )
        return res[:parts], res[parts:]

    def feed_fwd(layer, pieces, weights, tokens=()):
        res = call(
            functools.partial(feed_fwd_body, parts),
            block_out + [((total_rows, units), BF), ((total_rows, units), F32)],
            [*weights, vec[layer], *pieces],
            scalars=meta,
            vmem=24,
            tokens=tokens,
            name="feed_fwd",
        )
        return res[:parts], res[parts:]

    def mid_fwd(layer, x, terms, tokens=()):
        return call(
            functools.partial(mid_fwd_body, 3),
            [((rows, width), F32), ((rows, width), BF)],
            [x, vec[layer], *terms],
            tokens=tokens,
            name="mid_fwd",
        )

    out0, att0 = attend_fwd(0, a0, wattend0, [feed_slice0])
    wfeed0 = whole_pair(feed_slice0, [out0[0]])
    mid0, normed = mid_fwd(0, x0, scatter_rel(out0), [wfeed0[0]])
    wattend1 = whole_pair(layer_slice(attend_slices, 1, [wfeed0[0]]), [normed])
    c0 = gather_rel(normed)
    down0, feed0 = feed_fwd(0, c0, wfeed0, [wattend1[0]])
    wfeed1 = whole_pair(layer_slice(feed_slices, 1, [wattend1[0]]), [down0[0]])
    x1, normed = call(
        functools.partial(end_fwd_body, 3),
        [((rows, width), BF), ((rows, width), BF)],
        [mid0, vec[0], vec[1], *scatter_rel(down0)],
        tokens=[wfeed1[0]],
        name="end_fwd",
    )
    a1 = gather_rel(normed)
    cot = take_seat(lax.dynamic_index_in_dim(cotangent, section, 0, keepdims=False), 0)
    (grad1,) = call(
        masked_body, [((rows, width), BF)], [cot], scalars=meta, tokens=[a1[1]], name="masked"
    )
    g1 = gather_rel(grad1)
    out1, att1 = attend_fwd(1, a1, wattend1, [grad1])
    mid1, normed = mid_fwd(1, x1, scatter_rel(out1), [g1[1]])
    c1 = gather_rel(normed)
    down1, feed1 = feed_fwd(1, c1, wfeed1)

    def pick(first, second):
        return jnp.where(own_first, first, second), jnp.where(own_first, second, first)

    def collect(first, second):
        own, other = [leave_seat(t, flip) for flip, t in enumerate(pick(first, second))]
        (out,) = call(
            collect_body, [((2, rows, width), BF)], [own, other], scalars=meta, name="collect"
        )
        return out[None]

    def feed_back(g, weights, feed, tokens=()):
        res = call(
            functools.partial(feed_bwd_body, parts),
            block_out + [((total_rows, units), BF), ((1, units), F32)],
            [*weights, feed[1], *g],
            scalars=meta,
            vmem=24,
            tokens=tokens,
            name="feed_bwd",
        )
        return res[:parts], res[parts:]

    def feed_weights(c, g, feed, du):
        keep, send = call(
            functools.partial(feed_weights_body, parts),
            [((width, units), BF), ((width, units), BF)],
            [feed[0], du, *c, *g],
            scalars=meta,
            vmem=24,
            name="feed_weights",
        )
        return keep, swap_micro(send)

    def mid_back(layer, grad, mid, terms, tokens=()):
        return call(
            functools.partial(mid_bwd_body, 3),
            [((rows, width), F32), ((rows, width), BF), ((4, width), F32)],
            [grad, mid, vec[layer], *terms],
            tokens=tokens,
            name="mid_bwd",
        )

    def attend_back(hb, weights, att, tokens=()):
        res = call(
            functools.partial(attend_bwd_body, parts, slots),
            block_out + [tall, tall, tall, ((2, heads), F32)],
            [*weights, *att[:3], att[4], *hb],
            scalars=meta,
            scratch=[
                pltpu.VMEM((total_rows, heads), BF),
                pltpu.VMEM((heads // HD, total_rows, HD), F32),
                pltpu.VMEM((heads // HD, total_rows, HD), F32),
            ],
            vmem=24,
            tokens=tokens,
            name="attend_bwd",
        )
        return res[:parts], res[parts:]

    def attend_weights(a, hb, att, grads):
        keep, send = call(
            functools.partial(attend_weights_body, parts),
            [((width, 2 * heads), BF), ((width, 2 * heads), BF)],
            [att[3], *grads, *a, *hb],
            scalars=meta,
            vmem=24,
            name="attend_weights",
        )
        return keep, swap_micro(send)

    def end_back(layer, dmid, x, terms, tokens=()):
        return call(
            functools.partial(end_bwd_body, 3),
            [((rows, width), BF), ((2, width), F32)],
            [dmid, x, vec[layer], *terms],
            tokens=tokens,
            name="end_bwd",
        )

    up1, (du1, small_up1) = feed_back(g1, wfeed1, feed1)
    feed_pair1 = feed_weights(c1, g1, feed1, du1)
    dmid1, dlow, small_mid1 = mid_back(1, grad1, mid1, scatter_rel(up1), [feed_pair1[0]])
    hb1 = gather_rel(dlow)
    far, near = swap_rank(down1[3], 2), swap_rank(down1[2], 2)
    (chip,) = call(
        total_body, [((rows, width), BF)], [down1[1], far], tokens=[hb1[1]], name="chip_sum"
    )
    in1, (dq, dk, dv, small_qv1) = attend_back(hb1, wattend1, att1, [chip])
    (x2,) = call(
        functools.partial(last_fwd_body, 3),
        [((rows, width), BF)],
        [mid1, vec[1], down1[0], near, swap_rank(chip, 1)],
        tokens=[in1[0]],
        name="last_fwd",
    )
    attend_pair1 = attend_weights(a1, hb1, att1, (dq, dk, dv))
    blocks = pair_sum(*feed_pair1, meta, [in1[0]])
    layer_out = collect(x1, x2)
    dx1, small_end1 = end_back(
        1, dmid1, x1, scatter_rel(in1), [attend_pair1[0], blocks[0], x2]
    )
    g0 = gather_rel(dx1)
    up0, (du0, small_up0) = feed_back(g0, wfeed0, feed0)
    gfeed1 = sum_blocks(blocks, [up0[0]])
    blocks = pair_sum(*attend_pair1, meta, [up0[0]])
    feed_pair0 = feed_weights(c0, g0, feed0, du0)
    dmid0, dlow, small_mid0 = mid_back(
        0, dx1, mid0, scatter_rel(up0), [feed_pair0[0], blocks[0], gfeed1]
    )
    hb0 = gather_rel(dlow)
    early = sum_ranks(jnp.concatenate([small_end1, small_mid1, small_mid0], axis=0), [hb0[1]])
    feed_blocks = pair_sum(*feed_pair0, meta, [hb0[1]])
    in0, (dq, dk, dv, small_qv0) = attend_back(hb0, wattend0, att0, [feed_blocks[0], early, layer_out])
    gattend1 = sum_blocks(blocks, [in0[0]])
    attend_pair0 = attend_weights(a0, hb0, att0, (dq, dk, dv))
    early = sum_dp(
        jnp.concatenate([early, pad(small_up1), pad(small_qv1), pad(small_up0)], axis=0), [in0[0]]
    )
    dx0, small_end0 = end_back(
        0, dmid0, x0, scatter_rel(in0), [attend_pair0[0], gattend1, early]
    )
    blocks = pair_sum(*attend_pair0, meta)
    gfeed0 = sum_blocks(feed_blocks, [blocks[0]])
    gattend0 = sum_blocks(blocks)
    late = sum_dp(jnp.concatenate([sum_ranks(small_end0), pad(small_qv0)], axis=0))
    small0 = jnp.concatenate([late[:2], early[6:10], early[12:], late[2:]], axis=0)
    small1 = jnp.concatenate([early[:6], early[10:12]], axis=0)

    def to_owner(first, second):
        own, other = [leave_seat(t, flip) for flip, t in enumerate(pick(first, second))]
        return jnp.where(section == 0, own, other), jnp.where(section == 0, other, own)

    gup, gdown = [t.astype(F32) for t in to_owner(gfeed0, gfeed1)]
    gqk, gvo = [t.astype(F32) for t in to_owner(gattend0, gattend1)]
    gqkv = jnp.stack([gqk[:, :heads], gqk[:, heads:], gvo[:, :heads]])
    gout = gvo[:, heads:]

    input_grad = collect(dx0, dx1)

    mine = sum(leave_seat(t, flip) for flip, t in enumerate(pick(small0, small1)))
    return (
        layer_out,
        input_grad,
        jnp.stack([mine[0], mine[2]])[None],
        jnp.stack([mine[1], mine[3]])[None],
        gqkv[None],
        mine[7, : 2 * heads].reshape(1, 2, heads),
        gout.T[None],
        mine[4][None],
        gup[None],
        mine[6, :units][None],
        gdown.T[None],
        mine[5][None],
    )


def solution(mesh):
    in_specs = (
        P(None, ("dp", "tensor"), None),
        P(None, ("dp", "tensor"), None),
        P(None, "dp", None),
        P("section", None, None),
        P("section", None, None),
        P("section", None, "dp", "tensor"),
        P("section", None, "tensor"),
        P("section", "tensor", "dp"),
        P("section", None),
        P("section", "dp", "tensor"),
        P("section", "tensor"),
        P("section", "tensor", "dp"),
        P("section", None),
    )
    out_specs = (
        P("section", None, ("dp", "tensor"), None),
        P("section", None, ("dp", "tensor"), None),
        P("section", None, None),
        P("section", None, None),
        P("section", None, "dp", "tensor"),
        P("section", None, "tensor"),
        P("section", "tensor", "dp"),
        P("section", None),
        P("section", "dp", "tensor"),
        P("section", "tensor"),
        P("section", "tensor", "dp"),
        P("section", None),
    )
    return jax.shard_map(shards, mesh=mesh, in_specs=in_specs, out_specs=out_specs, check_vma=False)
```

```python
import functools

import jax
import jax.numpy as jnp
from jax import lax
from jax.experimental import pallas as pl
from jax.experimental.pallas import tpu as pltpu
from jax.sharding import PartitionSpec as P

HD = 64
BF = jnp.bfloat16
F32 = jnp.float32
VMEM = pl.BlockSpec(memory_space=pltpu.VMEM)
SMEM = pl.BlockSpec(memory_space=pltpu.SMEM)
MIB = 1 << 20

RANK, MICRO, DP, LAST, HALF, META = range(6)

GAIN0, GAIN1, SHIFT0, SHIFT1, B_OUT, B_DOWN, B_UP, B_QV = range(8)


def nn(left, right):
    return lax.dot_general(left, right, (((1,), (0,)), ((), ())), preferred_element_type=F32)


def nt(left, right):
    return lax.dot_general(left, right, (((1,), (1,)), ((), ())), preferred_element_type=F32)


def tn(left, right):
    return lax.dot_general(left, right, (((0,), (0,)), ((), ())), preferred_element_type=F32)


def call(
    body, outs, args, scalars=None, tokens=(), scratch=(), vmem=12, name=None, us=0.5
):
    args = ([] if scalars is None else [scalars]) + list(args)
    count = len(args)

    def kernel(*refs):
        body(*refs[:count], *refs[count + len(tokens) :])

    return pl.pallas_call(
        kernel,
        out_shape=[jax.ShapeDtypeStruct(s, d) for s, d in outs],
        in_specs=([] if scalars is None else [SMEM])
        + [VMEM] * (count - (scalars is not None))
        + [pl.BlockSpec(memory_space=pl.ANY)] * len(tokens),
        out_specs=[VMEM] * len(outs),
        scratch_shapes=list(scratch),
        compiler_params=pltpu.CompilerParams(vmem_limit_bytes=vmem * MIB),
        cost_estimate=pl.CostEstimate(flops=int(us * 1.15e9), bytes_accessed=1, transcendentals=0),
        name=name,
    )(*args, *tokens)


def swap(value, axis, by):
    count = lax.axis_size(axis)
    return lax.ppermute(value, axis, [(i, i ^ by) for i in range(count)])


def seat(micro, rank):
    half = lax.axis_size("tensor") // 2
    return rank // half * 2 * half + micro * half + rank % half


def permute(value, pairs):
    return lax.ppermute(value, ("section", "tensor"), pairs)


def seats():
    return [(m, r) for m in range(2) for r in range(lax.axis_size("tensor"))]


def swap_micro(value):
    return permute(value, [(seat(m, r), seat(1 - m, r)) for m, r in seats()])


def swap_rank(value, by):
    return permute(value, [(seat(m, r), seat(m, r ^ by)) for m, r in seats()])


def take_seat(value, flip):
    count = lax.axis_size("tensor")
    return permute(value, [((m ^ flip) * count + r, seat(m, r)) for m, r in seats()])


def leave_seat(value, flip):
    count = lax.axis_size("tensor")
    return permute(value, [(seat(m, r), (m ^ flip) * count + r) for m, r in seats()])


def gate(value, tokens):
    if not tokens:
        return value
    anywhere = pl.BlockSpec(memory_space=pl.ANY)

    def kernel(*refs):
        pass

    return pl.pallas_call(
        kernel,
        out_shape=jax.ShapeDtypeStruct(value.shape, value.dtype),
        in_specs=[anywhere] * (1 + len(tokens)),
        out_specs=anywhere,
        input_output_aliases={0: 0},
        compiler_params=pltpu.CompilerParams(vmem_limit_bytes=MIB),
        cost_estimate=pl.CostEstimate(flops=1, bytes_accessed=1, transcendentals=0),
        name="gate",
    )(value, *tokens)


def gather_rel(own, tokens=()):
    chip = gate(swap_rank(own, 1), tokens)
    return [own, chip, swap_rank(own, 2), swap_rank(chip, 2)]


def scatter_rel(parts, tokens=()):
    far = swap_rank(gate(parts[3], tokens), 2)
    near = swap_rank(parts[2], 2)
    (chip,) = call(total_body, [(far.shape, BF)], [parts[1], far], name="chip_sum")
    return [parts[0], near, swap_rank(chip, 1)], chip


def row_norm(x):
    mean = jnp.mean(x, axis=-1, keepdims=True)
    centred = x - mean
    var = jnp.mean(centred * centred, axis=-1, keepdims=True)
    inv = lax.rsqrt(var + 1e-05)
    return centred * inv, inv


def norm_back(grad, xhat, inv, gain):
    gx = grad * gain
    m1 = jnp.mean(gx, axis=-1, keepdims=True)
    m2 = jnp.mean(gx * xhat, axis=-1, keepdims=True)
    return inv * (gx - m1 - xhat * m2)


def add_terms(refs):
    total = refs[0][...].astype(F32)
    for ref in refs[1:]:
        total = total + ref[...].astype(F32)
    return total


def first_norm_body(x, vec, out):
    xhat, _ = row_norm(x[...].astype(F32))
    out[...] = (xhat * vec[GAIN0 : GAIN0 + 1, :] + vec[SHIFT0 : SHIFT0 + 1, :]).astype(BF)


def mid_fwd_body(parts, *refs):
    x, vec = refs[:2]
    terms = refs[2 : 2 + parts]
    mid, out = refs[2 + parts :]
    h = x[...].astype(F32) + add_terms(terms) + vec[B_OUT : B_OUT + 1, :]
    mid[...] = h
    xhat, _ = row_norm(h)
    out[...] = (xhat * vec[GAIN1 : GAIN1 + 1, :] + vec[SHIFT1 : SHIFT1 + 1, :]).astype(BF)


def end_fwd_body(parts, *refs):
    mid, vec, vec_next = refs[:3]
    terms = refs[3 : 3 + parts]
    result, out = refs[3 + parts :]
    y = (mid[...] + add_terms(terms) + vec[B_DOWN : B_DOWN + 1, :]).astype(BF)
    result[...] = y
    xhat, _ = row_norm(y.astype(F32))
    out[...] = (xhat * vec_next[GAIN0 : GAIN0 + 1, :] + vec_next[SHIFT0 : SHIFT0 + 1, :]).astype(BF)


def last_fwd_body(parts, *refs):
    mid, vec = refs[:2]
    terms = refs[2 : 2 + parts]
    (result,) = refs[2 + parts :]
    result[...] = (mid[...] + add_terms(terms) + vec[B_DOWN : B_DOWN + 1, :]).astype(BF)


def mid_bwd_body(parts, *refs):
    g, mid, vec = refs[:3]
    terms = refs[3 : 3 + parts]
    grad_mid, grad_low, small = refs[3 + parts :]
    grad = g[...].astype(F32)
    back = add_terms(terms)
    xhat, inv = row_norm(mid[...])
    dh = grad + norm_back(back, xhat, inv, vec[GAIN1 : GAIN1 + 1, :])
    grad_mid[...] = dh
    grad_low[...] = dh.astype(BF)
    small[0:1, :] = jnp.sum(back * xhat, axis=0, keepdims=True)
    small[1:2, :] = jnp.sum(back, axis=0, keepdims=True)
    small[2:3, :] = jnp.sum(dh, axis=0, keepdims=True)
    small[3:4, :] = jnp.sum(grad, axis=0, keepdims=True)


def end_bwd_body(parts, *refs):
    grad_mid, x, vec = refs[:3]
    terms = refs[3 : 3 + parts]
    result, small = refs[3 + parts :]
    back = add_terms(terms)
    xhat, inv = row_norm(x[...].astype(F32))
    result[...] = (grad_mid[...] + norm_back(back, xhat, inv, vec[GAIN0 : GAIN0 + 1, :])).astype(BF)
    small[0:1, :] = jnp.sum(back * xhat, axis=0, keepdims=True)
    small[1:2, :] = jnp.sum(back, axis=0, keepdims=True)


def chosen(flag, first, second):
    return jnp.where(flag == 0, first[...], second[...])


def ordered_rows(rank, by, block):
    return pl.ds(pl.multiple_of((rank ^ by) * block, 8), block)


def strip_mask(meta, slots, first, rows, cols):
    place = first + lax.broadcasted_iota(jnp.int32, (rows, 1), 0)
    start = jnp.zeros((rows, 1), jnp.int32)
    for s in range(slots):
        end = meta[META + s]
        start = jnp.where(place >= end, end, start)
    start = jnp.where(place >= meta[META + slots - 1], place, start)
    key = lax.broadcasted_iota(jnp.int32, (rows, cols), 1)
    return (key >= start) & (key <= place)


def attend_fwd_body(parts, slots, *refs):
    meta, own_w, other_w, vec = refs[:4]
    pieces = refs[4 : 4 + parts]
    outs = refs[4 + parts : 4 + 2 * parts]
    q, k, v, o, stat = refs[4 + 2 * parts :]
    rank = meta[RANK]
    block, width = pieces[0].shape[0], own_w.shape[1] // 2
    wqk = chosen(meta[MICRO], own_w, other_w)
    wvo = chosen(meta[MICRO], other_w, own_w)
    wq, wk, wv, wout = wqk[:, :width], wqk[:, width:], wvo[:, :width], wvo[:, width:]
    qb = vec[B_QV : B_QV + 1, :width]
    vb = vec[B_QV : B_QV + 1, width : 2 * width]
    for j in range(parts):
        rows = ordered_rows(rank, j, block)
        a = pieces[j][...]
        q[rows, :] = ((nn(a, wq) + qb) * (HD**-0.5)).astype(BF)
        k[rows, :] = nn(a, wk).astype(BF)
        v[rows, :] = (nn(a, wv) + vb).astype(BF)
    for i in range(parts):
        rows, cols = slice(i * block, (i + 1) * block), (i + 1) * block
        mask = strip_mask(meta, slots, i * block, block, cols)
        lane = lax.broadcasted_iota(jnp.int32, (block, 128), 1)
        stats = jnp.zeros((block, 128), F32)
        for h in range(width // HD):
            own = slice(h * HD, (h + 1) * HD)
            s = jnp.where(mask, nt(q[rows, own], k[:cols, own]), -1e9)
            top = jnp.max(s, axis=-1, keepdims=True)
            e = jnp.exp(s - top)
            total = jnp.sum(e, axis=-1, keepdims=True)
            p = (e * (1.0 / total)).astype(BF)
            o[rows, own] = nn(p, v[:cols, own]).astype(BF)
            stats = jnp.where(lane == h, top + jnp.log(total), stats)
        stat[rows, :] = stats
    for j in range(parts):
        outs[j][...] = nt(o[ordered_rows(rank, j, block), :], wout).astype(BF)


def attend_bwd_body(parts, slots, *refs):
    meta, own_w, other_w, q, k, v, stat = refs[:7]
    pieces = refs[7 : 7 + parts]
    outs = refs[7 + parts : 7 + 2 * parts]
    dq, dk, dv, small, do, dkf, dvf = refs[7 + 2 * parts :]
    rank = meta[RANK]
    block, width = pieces[0].shape[0], own_w.shape[1] // 2
    wqk = chosen(meta[MICRO], own_w, other_w)
    wvo = chosen(meta[MICRO], other_w, own_w)
    wq, wk, wv, wout = wqk[:, :width], wqk[:, width:], wvo[:, :width], wvo[:, width:]
    for j in range(parts):
        do[ordered_rows(rank, j, block), :] = nn(pieces[j][...], wout).astype(BF)
    for i in reversed(range(parts)):
        rows, cols = slice(i * block, (i + 1) * block), (i + 1) * block
        mask = strip_mask(meta, slots, i * block, block, cols)
        for h in range(width // HD):
            own = slice(h * HD, (h + 1) * HD)
            qh, kh, vh, doh = q[rows, own], k[:cols, own], v[:cols, own], do[rows, own]
            s = jnp.where(mask, nt(qh, kh), -1e9)
            p = jnp.exp(s - stat[rows, h : h + 1])
            dp = nt(doh, vh)
            inner = jnp.sum(dp * p, axis=-1, keepdims=True)
            ds = (p * (dp - inner)).astype(BF)
            dq[rows, own] = (nn(ds, kh).astype(BF).astype(F32) * (HD**-0.5)).astype(BF)
            dkh, dvh = tn(ds, qh), tn(p.astype(BF), doh)
            if i == parts - 1:
                dkf[h] = dkh
                dvf[h] = dvh
            else:
                dkf[h, :cols] += dkh
                dvf[h, :cols] += dvh
    for h in range(width // HD):
        own = slice(h * HD, (h + 1) * HD)
        dk[:, own] = dkf[h].astype(BF)
        dv[:, own] = dvf[h].astype(BF)
    small[0:1, :] = jnp.sum(dq[...].astype(F32), axis=0, keepdims=True)
    small[1:2, :] = jnp.sum(dv[...].astype(F32), axis=0, keepdims=True)
    for j in range(parts):
        rows = ordered_rows(rank, j, block)
        outs[j][...] = (nt(dq[rows, :], wq) + nt(dk[rows, :], wk) + nt(dv[rows, :], wv)).astype(BF)


def attend_weights_body(parts, *refs):
    meta, o, dq, dk, dv = refs[:5]
    normed = refs[5 : 5 + parts]
    grads = refs[5 + parts : 5 + 2 * parts]
    keep, send = refs[5 + 2 * parts :]
    rank, flag = meta[RANK], meta[MICRO]
    block, width = normed[0].shape[0], o.shape[1]
    totals = [None] * 4
    for j in range(parts):
        rows = ordered_rows(rank, j, block)
        a, g = normed[j][...], grads[j][...]
        terms = [tn(a, dq[rows, :]), tn(a, dk[rows, :]), tn(a, dv[rows, :]), tn(g, o[rows, :])]
        totals = [t if s is None else s + t for s, t in zip(totals, terms)]
    q, k, v, out = [t.astype(BF) for t in totals]
    keep[:, :width] = jnp.where(flag == 0, q, v)
    keep[:, width:] = jnp.where(flag == 0, k, out)
    send[:, :width] = jnp.where(flag == 0, v, q)
    send[:, width:] = jnp.where(flag == 0, out, k)


def feed_fwd_body(parts, *refs):
    meta, own_w, other_w, vec = refs[:4]
    pieces = refs[4 : 4 + parts]
    outs = refs[4 + parts : 4 + 2 * parts]
    hidden, slope = refs[4 + 2 * parts :]
    block = pieces[0].shape[0]
    wup = chosen(meta[MICRO], own_w, other_w)
    wdown = chosen(meta[MICRO], other_w, own_w)
    bias = vec[B_UP : B_UP + 1, : wup.shape[1]]
    for j in range(parts):
        rows = slice(j * block, (j + 1) * block)
        u = nn(pieces[j][...], wup) + bias
        share = 0.5 * (1.0 + lax.erf(u * (0.5**0.5)))
        f = (u * share).astype(BF)
        hidden[rows, :] = f
        slope[rows, :] = (share + u * (jnp.exp(-0.5 * (u * u)) * 0.3989422804014327)).astype(BF)
        outs[j][...] = nt(f, wdown).astype(BF)


def feed_bwd_body(parts, *refs):
    meta, own_w, other_w, slope = refs[:4]
    pieces = refs[4 : 4 + parts]
    outs = refs[4 + parts : 4 + 2 * parts]
    du, small = refs[4 + 2 * parts :]
    block = pieces[0].shape[0]
    wup = chosen(meta[MICRO], own_w, other_w)
    wdown = chosen(meta[MICRO], other_w, own_w)
    total = None
    for j in range(parts):
        rows = slice(j * block, (j + 1) * block)
        d = (nn(pieces[j][...], wdown) * slope[rows, :].astype(F32)).astype(BF)
        du[rows, :] = d
        term = jnp.sum(d.astype(F32), axis=0, keepdims=True)
        total = term if total is None else total + term
        outs[j][...] = nt(d, wup).astype(BF)
    small[...] = total


def feed_weights_body(parts, *refs):
    meta, hidden, du = refs[:3]
    normed = refs[3 : 3 + parts]
    grads = refs[3 + parts : 3 + 2 * parts]
    keep_a, keep_b, send_a, send_b = refs[3 + 2 * parts :]
    flag = meta[MICRO]
    block, half = normed[0].shape[0], keep_a.shape[1]
    up = down = None
    for j in range(parts):
        rows = slice(j * block, (j + 1) * block)
        t_up, t_down = tn(normed[j][...], du[rows, :]), tn(grads[j][...], hidden[rows, :])
        up, down = (t_up, t_down) if up is None else (up + t_up, down + t_down)
    up, down = up.astype(BF), down.astype(BF)
    keep_a[...] = jnp.where(flag == 0, up[:, :half], down[:, :half])
    keep_b[...] = jnp.where(flag == 0, up[:, half:], down[:, half:])
    send_a[...] = jnp.where(flag == 0, down[:, :half], up[:, :half])
    send_b[...] = jnp.where(flag == 0, down[:, half:], up[:, half:])


def layer_slice_body(layer, meta, own, other, out):
    out[...] = chosen(meta[MICRO] ^ layer, own, other)


def masked_body(meta, x, out):
    rows = x.shape[0]
    place = meta[RANK] * rows + lax.broadcasted_iota(jnp.int32, (rows, 1), 0)
    out[...] = jnp.where(place < meta[LAST], x[...].astype(F32), 0.0).astype(BF)


def assemble_body(meta, *refs):
    pieces, out = refs[:-1], refs[-1]
    size = pieces[0].shape[0]
    for k, piece in enumerate(pieces):
        out[ordered_rows(meta[DP], k, size), :] = piece[...]


def bit_of(meta, level):
    return (meta[DP] >> level) & 1


def join_body(level, meta, own, came, out):
    size = own.shape[0]
    bit = bit_of(meta, level)
    out[pl.ds(pl.multiple_of(bit * size, 8), size), :] = own[...]
    out[pl.ds(pl.multiple_of((1 - bit) * size, 8), size), :] = came[...]


def split_sum_body(level, meta, first, second, mine, send):
    size = mine.shape[0]
    bit = bit_of(meta, level)
    for part, out in ((bit, mine), (1 - bit, send)):
        rows = pl.ds(pl.multiple_of(part * size, 8), size)
        out[...] = (first[rows, :].astype(F32) + second[rows, :].astype(F32)).astype(out.dtype)


def pair_sum_body(meta, keep, came, *outs):
    size = outs[0].shape[0]
    for k, out in enumerate(outs):
        rows = ordered_rows(meta[DP], k, size)
        out[...] = (keep[rows, :].astype(F32) + came[rows, :].astype(F32)).astype(out.dtype)


def collect_body(meta, own, other, out):
    flag = jnp.where(meta[RANK] < meta[HALF], 0, 1)
    out[0] = chosen(flag, own, other)
    out[1] = chosen(flag, other, own)


def total_body(*refs):
    refs[-1][...] = add_terms(refs[:-1]).astype(refs[-1].dtype)


def gather_dp(shard, meta, tokens=()):
    count = lax.axis_size("dp")
    if count > 8:
        return lax.all_gather(shard, "dp", axis=0, tiled=True)
    pieces = [shard] + [swap(shard, "dp", k) for k in range(1, count)]
    shape = (shard.shape[0] * count, shard.shape[1])
    (whole,) = call(assemble_body, [(shape, BF)], pieces, scalars=meta, tokens=tokens, name="assemble")
    return whole


def pair_sum(keep, came, meta, tokens=()):
    count = lax.axis_size("dp")
    if count > 8:
        return [(keep.astype(F32) + came.astype(F32)).astype(BF)]
    shape = (keep.shape[0] // count, keep.shape[1])
    return call(
        pair_sum_body,
        [(shape, F32)] + [(shape, BF)] * (count - 1),
        [keep, came],
        scalars=meta,
        tokens=tokens,
        name="pair_sum",
    )


def sum_blocks(blocks, tokens=()):
    if len(blocks) == 1:
        return lax.psum_scatter(blocks[0], "dp", scatter_dimension=0, tiled=True)
    terms = [blocks[0]] + [swap(blocks[k], "dp", k) for k in range(1, len(blocks))]
    (total,) = call(total_body, [(blocks[0].shape, BF)], terms, tokens=tokens, name="total")
    return total


def join_dp(shard, level, meta, tokens=()):
    if lax.axis_size("dp") != 4:
        return lax.all_gather(shard, "dp", axis=0, tiled=True) if level else shard
    came = swap(shard, "dp", 1 << level)
    shape = (2 * shard.shape[0], shard.shape[1])
    (out,) = call(
        functools.partial(join_body, level),
        [(shape, BF)],
        [shard, came],
        scalars=meta,
        tokens=tokens,
        name="join",
    )
    return out


def split_dp(first, second, level, meta, tokens=()):
    if lax.axis_size("dp") != 4:
        both = first.astype(F32) + second.astype(F32)
        if level == 0:
            return both, jnp.zeros_like(both)
        both = lax.psum_scatter(both.astype(BF), "dp", scatter_dimension=0, tiled=True)
        return both, jnp.zeros_like(both)
    shape = (first.shape[0] // 2, first.shape[1])
    return call(
        functools.partial(split_sum_body, level),
        [(shape, F32), (shape, BF)],
        [first, second],
        scalars=meta,
        tokens=tokens,
        name="split_sum",
    )


def swap_level(value, level):
    return swap(value, "dp", 1 << level)


def add(first, second, tokens=()):
    (out,) = call(total_body, [(first.shape, BF)], [first, second], tokens=tokens, name="total")
    return out


def sum_dp(value, tokens=()):
    count = lax.axis_size("dp")
    if count > 8:
        return lax.psum(value, "dp")
    terms = [value] + [swap(value, "dp", k) for k in range(1, count)]
    (total,) = call(total_body, [(value.shape, F32)], terms, tokens=tokens, name="sum_dp")
    return total


def sum_ranks(value, tokens=()):
    terms = [value] + [swap_rank(value, k) for k in range(1, lax.axis_size("tensor"))]
    (total,) = call(total_body, [(value.shape, F32)], terms, tokens=tokens, name="sum_ranks")
    return total


def shards(
    inputs,
    cotangent,
    seq_lengths,
    norm_gain,
    norm_shift,
    w_qkv,
    b_qv,
    w_out,
    b_out,
    w_up,
    b_up,
    w_down,
    b_down,
):
    parts = lax.axis_size("tensor")
    section, place = lax.axis_index("section"), lax.axis_index("tensor")
    micro = place // (parts // 2)
    rank = section * (parts // 2) + place % (parts // 2)
    own_first = micro == 0
    rows, width = inputs.shape[1], inputs.shape[2]
    total_rows = rows * parts
    slots = seq_lengths.shape[2]
    heads = w_qkv.shape[3]
    units = w_up.shape[2]

    def by_layer(own, other):
        return jnp.where(own_first, own, other), jnp.where(own_first, other, own)

    def pad(row):
        return jnp.pad(row.reshape(1, -1), ((0, 0), (0, width - row.size)))

    lengths = lax.dynamic_index_in_dim(seq_lengths[:, 0], micro, 0, keepdims=False)
    ends = jnp.cumsum(lengths).astype(jnp.int32)
    meta = [rank, micro, lax.axis_index("dp"), ends[-1], parts // 2]
    meta = jnp.stack([jnp.asarray(m, jnp.int32) for m in meta])
    meta = jnp.concatenate([meta, ends])
    block_out = [((rows, width), BF)] * parts
    tall = ((total_rows, heads), BF)

    def slices_of(first, second, tokens=()):
        own, other = jnp.where(section == 0, first, second), jnp.where(section == 0, second, first)
        own, other = take_seat(gate(own, tokens), 0), take_seat(gate(other, tokens), 1)
        return own, other

    def layer_slice(slices, layer, tokens=()):
        (out,) = call(
            functools.partial(layer_slice_body, layer),
            [(slices[0].shape, BF)],
            slices,
            scalars=meta,
            tokens=tokens,
            name="layer_slice",
        )
        return out

    packed = jnp.concatenate(
        [norm_gain[0], norm_shift[0], b_out, b_down, pad(b_up[0]), pad(b_qv[0])], axis=0
    )
    attend_first = jnp.concatenate([w_qkv[0, 0], w_qkv[0, 1]], axis=1)
    attend_second = jnp.concatenate([w_qkv[0, 2], w_out[0].T], axis=1)
    attend_slices = slices_of(attend_first, attend_second)
    attend_slice0 = layer_slice(attend_slices, 0)
    x0 = lax.dynamic_index_in_dim(inputs, section, 0, keepdims=False)
    x0 = take_seat(gate(x0, [attend_slice0]), 0)
    packed = gate(packed, [attend_slice0])
    vec = by_layer(take_seat(packed, 0), take_seat(packed, 1))
    attend_own0 = gather_dp(attend_slice0, meta)
    (normed,) = call(first_norm_body, [((rows, width), BF)], [x0, vec[0]], name="norm_first")
    a0 = gather_rel(normed)
    feed_slices = slices_of(w_up[0], w_down[0].T, [normed])
    half = join_dp(layer_slice(feed_slices, 0, [attend_own0]), 0, meta)
    wattend0 = (attend_own0, swap_micro(attend_own0))

    def attend_fwd(layer, pieces, weights, tokens=()):
        res = call(
            functools.partial(attend_fwd_body, parts, slots),
            block_out + [tall, tall, tall, tall, ((total_rows, 128), F32)],
            [*weights, vec[layer], *pieces],
            scalars=meta,
            vmem=24,
            tokens=tokens,
            us=0.1,
            name="attend_fwd",
        )
        return res[:parts], res[parts:]

    def feed_fwd(layer, pieces, weights, tokens=()):
        res = call(
            functools.partial(feed_fwd_body, parts),
            block_out + [((total_rows, units), BF)] * 2,
            [*weights, vec[layer], *pieces],
            scalars=meta,
            vmem=24,
            tokens=tokens,
            us=0.1,
            name="feed_fwd",
        )
        return res[:parts], res[parts:]

    def mid_fwd(layer, x, terms, tokens=()):
        return call(
            functools.partial(mid_fwd_body, 3),
            [((rows, width), F32), ((rows, width), BF)],
            [x, vec[layer], *terms],
            tokens=tokens,
            name="mid_fwd",
        )

    out0, att0 = attend_fwd(0, a0, wattend0, [half])
    feed_own0 = join_dp(half, 1, meta, [out0[0]])
    terms = scatter_rel(out0, [feed_own0])
    wfeed0 = (feed_own0, swap_micro(feed_own0))
    half = join_dp(layer_slice(attend_slices, 1, [feed_own0]), 0, meta)
    mid0, normed = mid_fwd(0, x0, terms[0], [half])
    c0 = gather_rel(normed)
    down0, feed0 = feed_fwd(0, c0, wfeed0)
    attend_own1 = join_dp(half, 1, meta, [down0[0]])
    wattend1 = (attend_own1, swap_micro(attend_own1))
    half = join_dp(layer_slice(feed_slices, 1, [attend_own1]), 0, meta)
    x1, normed = call(
        functools.partial(end_fwd_body, 3),
        [((rows, width), BF), ((rows, width), BF)],
        [mid0, vec[0], vec[1], *scatter_rel(down0, [attend_own1])[0]],
        tokens=[half],
        name="end_fwd",
    )
    a1 = gather_rel(normed, [wattend1[1]])
    cot = lax.dynamic_index_in_dim(cotangent, section, 0, keepdims=False)
    cot = take_seat(gate(cot, [normed]), 0)
    (grad1,) = call(
        masked_body, [((rows, width), BF)], [cot], scalars=meta, tokens=[a1[1]], name="masked"
    )
    g1 = gather_rel(grad1)
    out1, att1 = attend_fwd(1, a1, wattend1, [grad1])
    feed_own1 = join_dp(half, 1, meta, [out1[0]])
    wfeed1 = (feed_own1, swap_micro(feed_own1))
    mid1, normed = mid_fwd(1, x1, scatter_rel(out1, [g1[1], feed_own1])[0])
    c1 = gather_rel(normed)
    down1, feed1 = feed_fwd(1, c1, wfeed1)

    def pick(first, second):
        return jnp.where(own_first, first, second), jnp.where(own_first, second, first)

    def collect(first, second, tokens=()):
        own, other = [leave_seat(t, flip) for flip, t in enumerate(pick(first, second))]
        (out,) = call(
            collect_body, [((2, rows, width), BF)], [own, other], scalars=meta, tokens=tokens, name="collect"
        )
        return out[None]

    def feed_back(g, weights, feed, tokens=()):
        res = call(
            functools.partial(feed_bwd_body, parts),
            block_out + [((total_rows, units), BF), ((1, units), F32)],
            [*weights, feed[1], *g],
            scalars=meta,
            vmem=24,
            tokens=tokens,
            us=3.5,
            name="feed_bwd",
        )
        return res[:parts], res[parts:]

    def feed_weights(c, g, feed, du):
        return call(
            functools.partial(feed_weights_body, parts),
            [((width, units // 2), BF)] * 4,
            [feed[0], du, *c, *g],
            scalars=meta,
            vmem=24,
            us=3.3,
            name="feed_weights",
        )

    def mid_back(layer, grad, mid, terms, tokens=()):
        return call(
            functools.partial(mid_bwd_body, 3),
            [((rows, width), F32), ((rows, width), BF), ((4, width), F32)],
            [grad, mid, vec[layer], *terms],
            tokens=tokens,
            name="mid_bwd",
        )

    def attend_back(hb, weights, att, tokens=()):
        res = call(
            functools.partial(attend_bwd_body, parts, slots),
            block_out + [tall, tall, tall, ((2, heads), F32)],
            [*weights, *att[:3], att[4], *hb],
            scalars=meta,
            scratch=[
                pltpu.VMEM((total_rows, heads), BF),
                pltpu.VMEM((heads // HD, total_rows, HD), F32),
                pltpu.VMEM((heads // HD, total_rows, HD), F32),
            ],
            vmem=24,
            tokens=tokens,
            us=0.1,
            name="attend_bwd",
        )
        return res[:parts], res[parts:]

    def attend_weights(a, hb, att, grads, tokens):
        return call(
            functools.partial(attend_weights_body, parts),
            [((width, 2 * heads), BF), ((width, 2 * heads), BF)],
            [att[3], *grads, *a, *hb],
            scalars=meta,
            vmem=24,
            us=2.5,
            tokens=tokens,
            name="attend_weights",
        )

    def end_back(layer, dmid, x, terms, tokens=()):
        return call(
            functools.partial(end_bwd_body, 3),
            [((rows, width), BF), ((2, width), F32)],
            [dmid, x, vec[layer], *terms],
            tokens=tokens,
            name="end_bwd",
        )

    up1, (du, small_up1) = feed_back(g1, wfeed1, feed1)
    keep_a, keep_b, send_a, send_b = feed_weights(c1, g1, feed1, du)
    dmid1, dlow, small_mid1 = mid_back(1, grad1, mid1, scatter_rel(up1)[0], [keep_a])
    came_a, came_b = swap_micro(send_a), swap_micro(send_b)
    hb1 = gather_rel(dlow, [came_a])
    far, near = swap_rank(down1[3], 2), swap_rank(down1[2], 2)
    (chip,) = call(
        total_body, [((rows, width), BF)], [down1[1], far], tokens=[hb1[1]], name="chip_sum"
    )
    mine_a, send_a = split_dp(keep_a, came_a, 1, meta)
    in1, (dq, dk, dv, small_qv1) = attend_back(hb1, wattend1, att1, [chip, mine_a])
    came_a = swap_level(send_a, 1)
    (x2,) = call(
        functools.partial(last_fwd_body, 3),
        [((rows, width), BF)],
        [mid1, vec[1], down1[0], near, swap_rank(chip, 1)],
        tokens=[in1[0]],
        name="last_fwd",
    )
    terms, chip = scatter_rel(in1, [came_b, came_a])
    mine_b, send_b = split_dp(keep_b, came_b, 1, meta, [chip])
    came_b = swap_level(send_b, 1)
    keep, send = attend_weights(a1, hb1, att1, (dq, dk, dv), [chip])
    dx1, small_end1 = end_back(1, dmid1, x1, terms, [keep, came_b, x2])
    came = swap_micro(send)
    mine_a, send_a = split_dp(mine_a, came_a, 0, meta, [dx1])
    mine_b, send_b = split_dp(mine_b, came_b, 0, meta, [dx1])
    came_a, came_b = swap_level(send_a, 0), swap_level(send_b, 0)
    g0 = gather_rel(dx1, [came, came_a, came_b])
    mine, send = split_dp(keep, came, 1, meta)
    gfeed1a, gfeed1b = add(mine_a, came_a), add(mine_b, came_b)

    up0, (du, small_up0) = feed_back(g0, wfeed0, feed0, [mine, gfeed1a, gfeed1b])
    came = swap_level(send, 1)
    keep_a, keep_b, send_a, send_b = feed_weights(c0, g0, feed0, du)
    dmid0, dlow, small_mid0 = mid_back(0, dx1, mid0, scatter_rel(up0)[0], [keep_a, came])
    mine, send = split_dp(mine, came, 0, meta, [dlow])
    came = swap_level(send, 0)
    came_a, came_b = swap_micro(send_a), swap_micro(send_b)
    hb0 = gather_rel(dlow, [came_a, came])
    gattend1 = add(mine, came)
    mine_a, send_a = split_dp(keep_a, came_a, 1, meta)
    late = gate(x2, [mine_a])
    in0, (dq, dk, dv, small_qv0) = attend_back(hb0, wattend0, att0, [mine_a, gattend1])
    layer_out = collect(x1, late, [in0[0]])
    came_a = swap_level(send_a, 1)
    terms, chip = scatter_rel(in0, [came_b, came_a])
    mine_b, send_b = split_dp(keep_b, came_b, 1, meta, [chip])
    mine_a, send_a = split_dp(mine_a, came_a, 0, meta, [chip])
    came_a, came_b = swap_level(send_a, 0), swap_level(send_b, 1)
    keep, send = attend_weights(a0, hb0, att0, (dq, dk, dv), [chip, layer_out])
    blocks = pair_sum(keep, swap_micro(send), meta)
    dx0, small_end0 = end_back(0, dmid0, x0, terms, [blocks[0]])
    gfeed0a = add(mine_a, came_a)
    mine_b, send_b = split_dp(mine_b, came_b, 0, meta, [dx0])
    gfeed0b = add(mine_b, swap_level(send_b, 0))
    gattend0 = sum_blocks(blocks)
    whole = sum_ranks(
        jnp.concatenate([small_end0, small_mid0, small_end1, small_mid1], axis=0)
    )
    whole = [whole[:6], pad(small_up0), pad(small_qv0), whole[6:], pad(small_up1), pad(small_qv1)]
    whole = sum_dp(jnp.concatenate(whole, axis=0))
    small0, small1 = whole[:8], whole[8:]

    def to_owner(first, second):
        own, other = [leave_seat(t, flip) for flip, t in enumerate(pick(first, second))]
        return jnp.where(section == 0, own, other), jnp.where(section == 0, other, own)

    gfeed0 = jnp.concatenate([gfeed0a, gfeed0b], axis=1)
    gfeed1 = jnp.concatenate([gfeed1a, gfeed1b], axis=1)
    gup, gdown = [t.astype(F32) for t in to_owner(gfeed0, gfeed1)]
    gqk, gvo = [t.astype(F32) for t in to_owner(gattend0, gattend1)]
    gqkv = jnp.stack([gqk[:, :heads], gqk[:, heads:], gvo[:, :heads]])
    gout = gvo[:, heads:]

    input_grad = collect(dx0, dx1)

    mine = sum(leave_seat(t, flip) for flip, t in enumerate(pick(small0, small1)))
    return (
        layer_out,
        input_grad,
        jnp.stack([mine[0], mine[2]])[None],
        jnp.stack([mine[1], mine[3]])[None],
        gqkv[None],
        mine[7, : 2 * heads].reshape(1, 2, heads),
        gout.T[None],
        mine[4][None],
        gup[None],
        mine[6, :units][None],
        gdown.T[None],
        mine[5][None],
    )


def solution(mesh):
    in_specs = (
        P(None, ("dp", "tensor"), None),
        P(None, ("dp", "tensor"), None),
        P(None, "dp", None),
        P("section", None, None),
        P("section", None, None),
        P("section", None, "dp", "tensor"),
        P("section", None, "tensor"),
        P("section", "tensor", "dp"),
        P("section", None),
        P("section", "dp", "tensor"),
        P("section", "tensor"),
        P("section", "tensor", "dp"),
        P("section", None),
    )
    out_specs = (
        P("section", None, ("dp", "tensor"), None),
        P("section", None, ("dp", "tensor"), None),
        P("section", None, None),
        P("section", None, None),
        P("section", None, "dp", "tensor"),
        P("section", None, "tensor"),
        P("section", "tensor", "dp"),
        P("section", None),
        P("section", "dp", "tensor"),
        P("section", "tensor"),
        P("section", "tensor", "dp"),
        P("section", None),
    )
    return jax.shard_map(shards, mesh=mesh, in_specs=in_specs, out_specs=out_specs, check_vma=False)
```

```python
import functools

import jax
import jax.numpy as jnp
from jax import lax
from jax.experimental import pallas as pl
from jax.experimental.pallas import tpu as pltpu
from jax.sharding import PartitionSpec as P

HD = 64
BF = jnp.bfloat16
F32 = jnp.float32
VMEM = pl.BlockSpec(memory_space=pltpu.VMEM)
SMEM = pl.BlockSpec(memory_space=pltpu.SMEM)
MIB = 1 << 20

RANK, MICRO, DP, LAST, HALF, META = range(6)

GAIN0, GAIN1, SHIFT0, SHIFT1, B_OUT, B_DOWN, B_UP, B_QV = range(8)


def nn(left, right):
    return lax.dot_general(left, right, (((1,), (0,)), ((), ())), preferred_element_type=F32)


def nt(left, right):
    return lax.dot_general(left, right, (((1,), (1,)), ((), ())), preferred_element_type=F32)


def tn(left, right):
    return lax.dot_general(left, right, (((0,), (0,)), ((), ())), preferred_element_type=F32)


def call(
    body, outs, args, scalars=None, tokens=(), scratch=(), vmem=12, name=None, us=0.5
):
    args = ([] if scalars is None else [scalars]) + list(args)
    count = len(args)

    def kernel(*refs):
        body(*refs[:count], *refs[count + len(tokens) :])

    return pl.pallas_call(
        kernel,
        out_shape=[jax.ShapeDtypeStruct(s, d) for s, d in outs],
        in_specs=([] if scalars is None else [SMEM])
        + [VMEM] * (count - (scalars is not None))
        + [pl.BlockSpec(memory_space=pl.ANY)] * len(tokens),
        out_specs=[VMEM] * len(outs),
        scratch_shapes=list(scratch),
        compiler_params=pltpu.CompilerParams(vmem_limit_bytes=vmem * MIB),
        cost_estimate=pl.CostEstimate(flops=int(us * 1.15e9), bytes_accessed=1, transcendentals=0),
        name=name,
    )(*args, *tokens)


def swap(value, axis, by):
    count = lax.axis_size(axis)
    return lax.ppermute(value, axis, [(i, i ^ by) for i in range(count)])


def seat(micro, rank):
    half = lax.axis_size("tensor") // 2
    return rank // half * 2 * half + micro * half + rank % half


def permute(value, pairs):
    return lax.ppermute(value, ("section", "tensor"), pairs)


def seats():
    return [(m, r) for m in range(2) for r in range(lax.axis_size("tensor"))]


def swap_micro(value):
    return permute(value, [(seat(m, r), seat(1 - m, r)) for m, r in seats()])


def swap_rank(value, by):
    return permute(value, [(seat(m, r), seat(m, r ^ by)) for m, r in seats()])


def take_seat(value, flip):
    count = lax.axis_size("tensor")
    return permute(value, [((m ^ flip) * count + r, seat(m, r)) for m, r in seats()])


def leave_seat(value, flip):
    count = lax.axis_size("tensor")
    return permute(value, [(seat(m, r), (m ^ flip) * count + r) for m, r in seats()])


def gate(value, tokens):
    if not tokens:
        return value
    anywhere = pl.BlockSpec(memory_space=pl.ANY)

    def kernel(*refs):
        pass

    return pl.pallas_call(
        kernel,
        out_shape=jax.ShapeDtypeStruct(value.shape, value.dtype),
        in_specs=[anywhere] * (1 + len(tokens)),
        out_specs=anywhere,
        input_output_aliases={0: 0},
        compiler_params=pltpu.CompilerParams(vmem_limit_bytes=MIB),
        cost_estimate=pl.CostEstimate(flops=1, bytes_accessed=1, transcendentals=0),
        name="gate",
    )(value, *tokens)


def gather_rel(own, tokens=()):
    chip = gate(swap_rank(own, 1), tokens)
    return [own, chip, swap_rank(own, 2), swap_rank(chip, 2)]


def scatter_rel(parts, tokens=()):
    far = swap_rank(gate(parts[3], tokens), 2)
    near = swap_rank(parts[2], 2)
    (chip,) = call(total_body, [(far.shape, BF)], [parts[1], far], name="chip_sum")
    return [parts[0], near, swap_rank(chip, 1)], chip


def row_norm(x):
    mean = jnp.mean(x, axis=-1, keepdims=True)
    centred = x - mean
    var = jnp.mean(centred * centred, axis=-1, keepdims=True)
    inv = lax.rsqrt(var + 1e-05)
    return centred * inv, inv


def norm_back(grad, xhat, inv, gain):
    gx = grad * gain
    m1 = jnp.mean(gx, axis=-1, keepdims=True)
    m2 = jnp.mean(gx * xhat, axis=-1, keepdims=True)
    return inv * (gx - m1 - xhat * m2)


def add_terms(refs):
    total = refs[0][...].astype(F32)
    for ref in refs[1:]:
        total = total + ref[...].astype(F32)
    return total


def first_norm_body(x, vec, out):
    xhat, _ = row_norm(x[...].astype(F32))
    out[...] = (xhat * vec[GAIN0 : GAIN0 + 1, :] + vec[SHIFT0 : SHIFT0 + 1, :]).astype(BF)


def mid_fwd_body(parts, *refs):
    x, vec = refs[:2]
    terms = refs[2 : 2 + parts]
    mid, out = refs[2 + parts :]
    h = x[...].astype(F32) + add_terms(terms) + vec[B_OUT : B_OUT + 1, :]
    mid[...] = h
    xhat, _ = row_norm(h)
    out[...] = (xhat * vec[GAIN1 : GAIN1 + 1, :] + vec[SHIFT1 : SHIFT1 + 1, :]).astype(BF)


def end_fwd_body(parts, *refs):
    mid, vec, vec_next = refs[:3]
    terms = refs[3 : 3 + parts]
    result, out = refs[3 + parts :]
    y = (mid[...] + add_terms(terms) + vec[B_DOWN : B_DOWN + 1, :]).astype(BF)
    result[...] = y
    xhat, _ = row_norm(y.astype(F32))
    out[...] = (xhat * vec_next[GAIN0 : GAIN0 + 1, :] + vec_next[SHIFT0 : SHIFT0 + 1, :]).astype(BF)


def last_fwd_body(parts, *refs):
    mid, vec = refs[:2]
    terms = refs[2 : 2 + parts]
    (result,) = refs[2 + parts :]
    result[...] = (mid[...] + add_terms(terms) + vec[B_DOWN : B_DOWN + 1, :]).astype(BF)


def mid_bwd_body(parts, *refs):
    g, mid, vec = refs[:3]
    terms = refs[3 : 3 + parts]
    grad_mid, grad_low, small = refs[3 + parts :]
    grad = g[...].astype(F32)
    back = add_terms(terms)
    xhat, inv = row_norm(mid[...])
    dh = grad + norm_back(back, xhat, inv, vec[GAIN1 : GAIN1 + 1, :])
    grad_mid[...] = dh
    grad_low[...] = dh.astype(BF)
    small[0:1, :] = jnp.sum(back * xhat, axis=0, keepdims=True)
    small[1:2, :] = jnp.sum(back, axis=0, keepdims=True)
    small[2:3, :] = jnp.sum(dh, axis=0, keepdims=True)
    small[3:4, :] = jnp.sum(grad, axis=0, keepdims=True)


def end_bwd_body(parts, *refs):
    grad_mid, x, vec = refs[:3]
    terms = refs[3 : 3 + parts]
    result, small = refs[3 + parts :]
    back = add_terms(terms)
    xhat, inv = row_norm(x[...].astype(F32))
    result[...] = (grad_mid[...] + norm_back(back, xhat, inv, vec[GAIN0 : GAIN0 + 1, :])).astype(BF)
    small[0:1, :] = jnp.sum(back * xhat, axis=0, keepdims=True)
    small[1:2, :] = jnp.sum(back, axis=0, keepdims=True)


def chosen(flag, first, second):
    return jnp.where(flag == 0, first[...], second[...])


def ordered_rows(rank, by, block):
    return pl.ds(pl.multiple_of((rank ^ by) * block, 8), block)


def strip_mask(meta, slots, first, rows, cols):
    place = first + lax.broadcasted_iota(jnp.int32, (rows, 1), 0)
    start = jnp.zeros((rows, 1), jnp.int32)
    for s in range(slots):
        end = meta[META + s]
        start = jnp.where(place >= end, end, start)
    start = jnp.where(place >= meta[META + slots - 1], place, start)
    key = lax.broadcasted_iota(jnp.int32, (rows, cols), 1)
    return (key >= start) & (key <= place)


def attend_fwd_body(parts, slots, *refs):
    meta, own_w, other_w, vec = refs[:4]
    pieces = refs[4 : 4 + parts]
    outs = refs[4 + parts : 4 + 2 * parts]
    q, k, v, o, stat = refs[4 + 2 * parts :]
    rank = meta[RANK]
    block, width = pieces[0].shape[0], own_w.shape[1] // 2
    wqk = chosen(meta[MICRO], own_w, other_w)
    wvo = chosen(meta[MICRO], other_w, own_w)
    wq, wk, wv, wout = wqk[:, :width], wqk[:, width:], wvo[:, :width], wvo[:, width:]
    qb = vec[B_QV : B_QV + 1, :width]
    vb = vec[B_QV : B_QV + 1, width : 2 * width]
    for j in range(parts):
        rows = ordered_rows(rank, j, block)
        a = pieces[j][...]
        q[rows, :] = ((nn(a, wq) + qb) * (HD**-0.5)).astype(BF)
        k[rows, :] = nn(a, wk).astype(BF)
        v[rows, :] = (nn(a, wv) + vb).astype(BF)
    for i in range(parts):
        rows, cols = slice(i * block, (i + 1) * block), (i + 1) * block
        mask = strip_mask(meta, slots, i * block, block, cols)
        lane = lax.broadcasted_iota(jnp.int32, (block, 128), 1)
        stats = jnp.zeros((block, 128), F32)
        for h in range(width // HD):
            own = slice(h * HD, (h + 1) * HD)
            s = jnp.where(mask, nt(q[rows, own], k[:cols, own]), -1e9)
            top = jnp.max(s, axis=-1, keepdims=True)
            e = jnp.exp(s - top)
            total = jnp.sum(e, axis=-1, keepdims=True)
            p = (e * (1.0 / total)).astype(BF)
            o[rows, own] = nn(p, v[:cols, own]).astype(BF)
            stats = jnp.where(lane == h, top + jnp.log(total), stats)
        stat[rows, :] = stats
    for j in range(parts):
        outs[j][...] = nt(o[ordered_rows(rank, j, block), :], wout).astype(BF)


def attend_bwd_body(parts, slots, *refs):
    meta, own_w, other_w, q, k, v, stat = refs[:7]
    pieces = refs[7 : 7 + parts]
    outs = refs[7 + parts : 7 + 2 * parts]
    dq, dk, dv, small, do, dkf, dvf = refs[7 + 2 * parts :]
    rank = meta[RANK]
    block, width = pieces[0].shape[0], own_w.shape[1] // 2
    wqk = chosen(meta[MICRO], own_w, other_w)
    wvo = chosen(meta[MICRO], other_w, own_w)
    wq, wk, wv, wout = wqk[:, :width], wqk[:, width:], wvo[:, :width], wvo[:, width:]
    for j in range(parts):
        do[ordered_rows(rank, j, block), :] = nn(pieces[j][...], wout).astype(BF)
    for i in reversed(range(parts)):
        rows, cols = slice(i * block, (i + 1) * block), (i + 1) * block
        mask = strip_mask(meta, slots, i * block, block, cols)
        for h in range(width // HD):
            own = slice(h * HD, (h + 1) * HD)
            qh, kh, vh, doh = q[rows, own], k[:cols, own], v[:cols, own], do[rows, own]
            s = jnp.where(mask, nt(qh, kh), -1e9)
            p = jnp.exp(s - stat[rows, h : h + 1])
            dp = nt(doh, vh)
            inner = jnp.sum(dp * p, axis=-1, keepdims=True)
            ds = (p * (dp - inner)).astype(BF)
            dq[rows, own] = (nn(ds, kh).astype(BF).astype(F32) * (HD**-0.5)).astype(BF)
            dkh, dvh = tn(ds, qh), tn(p.astype(BF), doh)
            if i == parts - 1:
                dkf[h] = dkh
                dvf[h] = dvh
            else:
                dkf[h, :cols] += dkh
                dvf[h, :cols] += dvh
    for h in range(width // HD):
        own = slice(h * HD, (h + 1) * HD)
        dk[:, own] = dkf[h].astype(BF)
        dv[:, own] = dvf[h].astype(BF)
    small[0:1, :] = jnp.sum(dq[...].astype(F32), axis=0, keepdims=True)
    small[1:2, :] = jnp.sum(dv[...].astype(F32), axis=0, keepdims=True)
    for j in range(parts):
        rows = ordered_rows(rank, j, block)
        outs[j][...] = (nt(dq[rows, :], wq) + nt(dk[rows, :], wk) + nt(dv[rows, :], wv)).astype(BF)


def attend_weights_body(parts, *refs):
    meta, o, dq, dk, dv = refs[:5]
    normed = refs[5 : 5 + parts]
    grads = refs[5 + parts : 5 + 2 * parts]
    keep, send = refs[5 + 2 * parts :]
    rank, flag = meta[RANK], meta[MICRO]
    block, width = normed[0].shape[0], o.shape[1]
    totals = [None] * 4
    for j in range(parts):
        rows = ordered_rows(rank, j, block)
        a, g = normed[j][...], grads[j][...]
        terms = [tn(a, dq[rows, :]), tn(a, dk[rows, :]), tn(a, dv[rows, :]), tn(g, o[rows, :])]
        totals = [t if s is None else s + t for s, t in zip(totals, terms)]
    q, k, v, out = [t.astype(BF) for t in totals]
    keep[:, :width] = jnp.where(flag == 0, q, v)
    keep[:, width:] = jnp.where(flag == 0, k, out)
    send[:, :width] = jnp.where(flag == 0, v, q)
    send[:, width:] = jnp.where(flag == 0, out, k)


def feed_fwd_body(parts, *refs):
    meta, own_w, other_w, vec = refs[:4]
    pieces = refs[4 : 4 + parts]
    outs = refs[4 + parts : 4 + 2 * parts]
    hidden, slope = refs[4 + 2 * parts :]
    block = pieces[0].shape[0]
    wup = chosen(meta[MICRO], own_w, other_w)
    wdown = chosen(meta[MICRO], other_w, own_w)
    bias = vec[B_UP : B_UP + 1, : wup.shape[1]]
    for j in range(parts):
        rows = slice(j * block, (j + 1) * block)
        u = nn(pieces[j][...], wup) + bias
        share = 0.5 * (1.0 + lax.erf(u * (0.5**0.5)))
        f = (u * share).astype(BF)
        hidden[rows, :] = f
        slope[rows, :] = (share + u * (jnp.exp(-0.5 * (u * u)) * 0.3989422804014327)).astype(BF)
        outs[j][...] = nt(f, wdown).astype(BF)


def feed_bwd_body(parts, *refs):
    meta, own_w, other_w, slope = refs[:4]
    pieces = refs[4 : 4 + parts]
    outs = refs[4 + parts : 4 + 2 * parts]
    du, small = refs[4 + 2 * parts :]
    block = pieces[0].shape[0]
    wup = chosen(meta[MICRO], own_w, other_w)
    wdown = chosen(meta[MICRO], other_w, own_w)
    total = None
    for j in range(parts):
        rows = slice(j * block, (j + 1) * block)
        d = (nn(pieces[j][...], wdown) * slope[rows, :].astype(F32)).astype(BF)
        du[rows, :] = d
        term = jnp.sum(d.astype(F32), axis=0, keepdims=True)
        total = term if total is None else total + term
        outs[j][...] = nt(d, wup).astype(BF)
    small[...] = total


def feed_weights_body(parts, *refs):
    meta, hidden, du = refs[:3]
    normed = refs[3 : 3 + parts]
    grads = refs[3 + parts : 3 + 2 * parts]
    keep_a, keep_b, send_a, send_b = refs[3 + 2 * parts :]
    flag = meta[MICRO]
    block, half = normed[0].shape[0], keep_a.shape[1]
    up = down = None
    for j in range(parts):
        rows = slice(j * block, (j + 1) * block)
        t_up, t_down = tn(normed[j][...], du[rows, :]), tn(grads[j][...], hidden[rows, :])
        up, down = (t_up, t_down) if up is None else (up + t_up, down + t_down)
    up, down = up.astype(BF), down.astype(BF)
    keep_a[...] = jnp.where(flag == 0, up[:, :half], down[:, :half])
    keep_b[...] = jnp.where(flag == 0, up[:, half:], down[:, half:])
    send_a[...] = jnp.where(flag == 0, down[:, :half], up[:, :half])
    send_b[...] = jnp.where(flag == 0, down[:, half:], up[:, half:])


def layer_slice_body(layer, meta, own, other, out):
    out[...] = chosen(meta[MICRO] ^ layer, own, other)


def masked_body(meta, x, out):
    rows = x.shape[0]
    place = meta[RANK] * rows + lax.broadcasted_iota(jnp.int32, (rows, 1), 0)
    out[...] = jnp.where(place < meta[LAST], x[...].astype(F32), 0.0).astype(BF)


def assemble_body(meta, *refs):
    pieces, out = refs[:-1], refs[-1]
    size = pieces[0].shape[0]
    for k, piece in enumerate(pieces):
        out[ordered_rows(meta[DP], k, size), :] = piece[...]


def bit_of(meta, level):
    return (meta[DP] >> level) & 1


def join_body(level, meta, own, came, out):
    size = own.shape[0]
    bit = bit_of(meta, level)
    out[pl.ds(pl.multiple_of(bit * size, 8), size), :] = own[...]
    out[pl.ds(pl.multiple_of((1 - bit) * size, 8), size), :] = came[...]


def split_sum_body(level, meta, first, second, mine, send):
    size = mine.shape[0]
    bit = bit_of(meta, level)
    for part, out in ((bit, mine), (1 - bit, send)):
        rows = pl.ds(pl.multiple_of(part * size, 8), size)
        out[...] = (first[rows, :].astype(F32) + second[rows, :].astype(F32)).astype(out.dtype)


def pair_sum_body(meta, keep, came, *outs):
    size = outs[0].shape[0]
    for k, out in enumerate(outs):
        rows = ordered_rows(meta[DP], k, size)
        out[...] = (keep[rows, :].astype(F32) + came[rows, :].astype(F32)).astype(out.dtype)


def collect_body(meta, own, other, out):
    flag = jnp.where(meta[RANK] < meta[HALF], 0, 1)
    out[0] = chosen(flag, own, other)
    out[1] = chosen(flag, other, own)


def finish_feed_body(meta, own, other, up, down):
    flag = jnp.where(meta[RANK] < meta[HALF], 0, 1)
    up[...] = chosen(flag, own, other).astype(F32)
    down[...] = chosen(flag, other, own).astype(F32).T


def finish_attend_body(meta, own, other, qkv, out):
    flag = jnp.where(meta[RANK] < meta[HALF], 0, 1)
    width = out.shape[0]
    first = chosen(flag, own, other).astype(F32)
    second = chosen(flag, other, own).astype(F32)
    qkv[0] = first[:, :width]
    qkv[1] = first[:, width:]
    qkv[2] = second[:, :width]
    out[...] = second[:, width:].T


def total_body(*refs):
    refs[-1][...] = add_terms(refs[:-1]).astype(refs[-1].dtype)


def gather_dp(shard, meta, tokens=()):
    count = lax.axis_size("dp")
    if count > 8:
        return lax.all_gather(shard, "dp", axis=0, tiled=True), shard
    pieces = [shard] + [swap(shard, "dp", k) for k in range(1, count)]
    shape = (shard.shape[0] * count, shard.shape[1])
    (whole,) = call(assemble_body, [(shape, BF)], pieces, scalars=meta, tokens=tokens, name="assemble")
    return whole, pieces[1]


def pair_sum(keep, came, meta, tokens=()):
    count = lax.axis_size("dp")
    if count > 8:
        return [(keep.astype(F32) + came.astype(F32)).astype(BF)]
    shape = (keep.shape[0] // count, keep.shape[1])
    return call(
        pair_sum_body,
        [(shape, F32)] + [(shape, BF)] * (count - 1),
        [keep, came],
        scalars=meta,
        tokens=tokens,
        name="pair_sum",
    )


def sum_blocks(blocks, tokens=()):
    if len(blocks) == 1:
        return lax.psum_scatter(blocks[0], "dp", scatter_dimension=0, tiled=True)
    terms = [blocks[0]] + [swap(blocks[k], "dp", k) for k in range(1, len(blocks))]
    (total,) = call(total_body, [(blocks[0].shape, BF)], terms, tokens=tokens, name="total")
    return total


def join_dp(shard, level, meta, tokens=()):
    if lax.axis_size("dp") != 4:
        return lax.all_gather(shard, "dp", axis=0, tiled=True) if level else shard
    came = swap(shard, "dp", 1 << level)
    shape = (2 * shard.shape[0], shard.shape[1])
    (out,) = call(
        functools.partial(join_body, level),
        [(shape, BF)],
        [shard, came],
        scalars=meta,
        tokens=tokens,
        name="join",
    )
    return out


def split_dp(first, second, level, meta, tokens=()):
    if lax.axis_size("dp") != 4:
        both = first.astype(F32) + second.astype(F32)
        if level == 0:
            return both, jnp.zeros_like(both)
        both = lax.psum_scatter(both.astype(BF), "dp", scatter_dimension=0, tiled=True)
        return both, jnp.zeros_like(both)
    shape = (first.shape[0] // 2, first.shape[1])
    return call(
        functools.partial(split_sum_body, level),
        [(shape, F32), (shape, BF)],
        [first, second],
        scalars=meta,
        tokens=tokens,
        name="split_sum",
    )


def swap_level(value, level):
    return swap(value, "dp", 1 << level)


def add(first, second, tokens=()):
    (out,) = call(total_body, [(first.shape, BF)], [first, second], tokens=tokens, name="total")
    return out


def sum_dp(value, tokens=()):
    count = lax.axis_size("dp")
    if count > 8:
        return lax.psum(value, "dp")
    by = 1
    while by < count:
        terms = [value, swap(value, "dp", by)]
        (value,) = call(total_body, [(value.shape, F32)], terms, tokens=tokens, name="sum_dp")
        by *= 2
    return value


def sum_ranks(value, tokens=()):
    by = 1
    while by < lax.axis_size("tensor"):
        terms = [value, swap_rank(value, by)]
        (value,) = call(total_body, [(value.shape, F32)], terms, tokens=tokens, name="sum_ranks")
        by *= 2
    return value


def shards(
    inputs,
    cotangent,
    seq_lengths,
    norm_gain,
    norm_shift,
    w_qkv,
    b_qv,
    w_out,
    b_out,
    w_up,
    b_up,
    w_down,
    b_down,
):
    parts = lax.axis_size("tensor")
    section, place = lax.axis_index("section"), lax.axis_index("tensor")
    micro = place // (parts // 2)
    rank = section * (parts // 2) + place % (parts // 2)
    own_first = micro == 0
    rows, width = inputs.shape[1], inputs.shape[2]
    total_rows = rows * parts
    slots = seq_lengths.shape[2]
    heads = w_qkv.shape[3]
    units = w_up.shape[2]

    def by_layer(own, other):
        return jnp.where(own_first, own, other), jnp.where(own_first, other, own)

    def pad(row):
        return jnp.pad(row.reshape(1, -1), ((0, 0), (0, width - row.size)))

    lengths = lax.dynamic_index_in_dim(seq_lengths[:, 0], micro, 0, keepdims=False)
    ends = jnp.cumsum(lengths).astype(jnp.int32)
    meta = [rank, micro, lax.axis_index("dp"), ends[-1], parts // 2]
    meta = jnp.stack([jnp.asarray(m, jnp.int32) for m in meta])
    meta = jnp.concatenate([meta, ends])
    block_out = [((rows, width), BF)] * parts
    tall = ((total_rows, heads), BF)

    def slices_of(first, second, tokens=()):
        own, other = jnp.where(section == 0, first, second), jnp.where(section == 0, second, first)
        own, other = take_seat(gate(own, tokens), 0), take_seat(gate(other, tokens), 1)
        return own, other

    def layer_slice(slices, layer, tokens=()):
        (out,) = call(
            functools.partial(layer_slice_body, layer),
            [(slices[0].shape, BF)],
            slices,
            scalars=meta,
            tokens=tokens,
            name="layer_slice",
        )
        return out

    packed = jnp.concatenate(
        [norm_gain[0], norm_shift[0], b_out, b_down, pad(b_up[0]), pad(b_qv[0])], axis=0
    )
    attend_first = jnp.concatenate([w_qkv[0, 0], w_qkv[0, 1]], axis=1)
    attend_second = jnp.concatenate([w_qkv[0, 2], w_out[0].T], axis=1)
    attend_slices = slices_of(attend_first, attend_second)
    x0 = take_seat(lax.dynamic_index_in_dim(inputs, section, 0, keepdims=False), 0)
    vec = by_layer(take_seat(packed, 0), take_seat(packed, 1))
    attend_slice0 = layer_slice(attend_slices, 0, [x0, vec[0]])
    attend_own0, first_piece = gather_dp(attend_slice0, meta)
    (normed,) = call(first_norm_body, [((rows, width), BF)], [x0, vec[0]], name="norm_first")
    a0 = gather_rel(normed)
    feed_slices = slices_of(w_up[0], w_down[0].T, [first_piece])
    half = join_dp(layer_slice(feed_slices, 0, [attend_own0]), 0, meta)
    wattend0 = (attend_own0, swap_micro(attend_own0))

    def attend_fwd(layer, pieces, weights, tokens=()):
        res = call(
            functools.partial(attend_fwd_body, parts, slots),
            block_out + [tall, tall, tall, tall, ((total_rows, 128), F32)],
            [*weights, vec[layer], *pieces],
            scalars=meta,
            vmem=24,
            tokens=tokens,
            us=0.1,
            name="attend_fwd",
        )
        return res[:parts], res[parts:]

    def feed_fwd(layer, pieces, weights, tokens=()):
        res = call(
            functools.partial(feed_fwd_body, parts),
            block_out + [((total_rows, units), BF)] * 2,
            [*weights, vec[layer], *pieces],
            scalars=meta,
            vmem=24,
            tokens=tokens,
            us=0.1,
            name="feed_fwd",
        )
        return res[:parts], res[parts:]

    def mid_fwd(layer, x, terms, tokens=()):
        return call(
            functools.partial(mid_fwd_body, 3),
            [((rows, width), F32), ((rows, width), BF)],
            [x, vec[layer], *terms],
            tokens=tokens,
            name="mid_fwd",
        )

    out0, att0 = attend_fwd(0, a0, wattend0, [half])
    terms, chip = scatter_rel(out0)
    feed_own0 = join_dp(half, 1, meta, [chip])
    mid0, normed = mid_fwd(0, x0, terms, [feed_own0])
    wfeed0 = (feed_own0, swap_micro(feed_own0))
    half = join_dp(layer_slice(attend_slices, 1, [feed_own0]), 0, meta)
    c0 = gather_rel(normed, [half])
    attend_own1 = join_dp(half, 1, meta)
    down0, feed0 = feed_fwd(0, c0, wfeed0, [attend_own1])
    wattend1 = (attend_own1, swap_micro(attend_own1))
    half = join_dp(layer_slice(feed_slices, 1, [attend_own1]), 0, meta)
    x1, normed = call(
        functools.partial(end_fwd_body, 3),
        [((rows, width), BF), ((rows, width), BF)],
        [mid0, vec[0], vec[1], *scatter_rel(down0)[0]],
        tokens=[half],
        name="end_fwd",
    )
    a1 = gather_rel(normed, [wattend1[1]])
    cot = lax.dynamic_index_in_dim(cotangent, section, 0, keepdims=False)
    cot = take_seat(gate(cot, [normed]), 0)
    (grad1,) = call(
        masked_body, [((rows, width), BF)], [cot], scalars=meta, tokens=[a1[1]], name="masked"
    )
    g1 = gather_rel(grad1)
    out1, att1 = attend_fwd(1, a1, wattend1, [grad1])
    feed_own1 = join_dp(half, 1, meta, [out1[0]])
    wfeed1 = (feed_own1, swap_micro(feed_own1))
    mid1, normed = mid_fwd(1, x1, scatter_rel(out1, [g1[1], feed_own1])[0])
    c1 = gather_rel(normed)
    down1, feed1 = feed_fwd(1, c1, wfeed1)

    def pick(first, second):
        return jnp.where(own_first, first, second), jnp.where(own_first, second, first)

    def collect(first, second, tokens=()):
        own, other = [leave_seat(t, flip) for flip, t in enumerate(pick(first, second))]
        (out,) = call(
            collect_body, [((2, rows, width), BF)], [own, other], scalars=meta, tokens=tokens, name="collect"
        )
        return out[None]

    def feed_back(g, weights, feed, tokens=()):
        res = call(
            functools.partial(feed_bwd_body, parts),
            block_out + [((total_rows, units), BF), ((1, units), F32)],
            [*weights, feed[1], *g],
            scalars=meta,
            vmem=24,
            tokens=tokens,
            us=3.5,
            name="feed_bwd",
        )
        return res[:parts], res[parts:]

    def feed_weights(c, g, feed, du):
        return call(
            functools.partial(feed_weights_body, parts),
            [((width, units // 2), BF)] * 4,
            [feed[0], du, *c, *g],
            scalars=meta,
            vmem=24,
            us=3.3,
            name="feed_weights",
        )

    def mid_back(layer, grad, mid, terms, tokens=()):
        return call(
            functools.partial(mid_bwd_body, 3),
            [((rows, width), F32), ((rows, width), BF), ((4, width), F32)],
            [grad, mid, vec[layer], *terms],
            tokens=tokens,
            name="mid_bwd",
        )

    def attend_back(hb, weights, att, tokens=()):
        res = call(
            functools.partial(attend_bwd_body, parts, slots),
            block_out + [tall, tall, tall, ((2, heads), F32)],
            [*weights, *att[:3], att[4], *hb],
            scalars=meta,
            scratch=[
                pltpu.VMEM((total_rows, heads), BF),
                pltpu.VMEM((heads // HD, total_rows, HD), F32),
                pltpu.VMEM((heads // HD, total_rows, HD), F32),
            ],
            vmem=24,
            tokens=tokens,
            us=0.1,
            name="attend_bwd",
        )
        return res[:parts], res[parts:]

    def attend_weights(a, hb, att, grads, tokens):
        return call(
            functools.partial(attend_weights_body, parts),
            [((width, 2 * heads), BF), ((width, 2 * heads), BF)],
            [att[3], *grads, *a, *hb],
            scalars=meta,
            vmem=24,
            us=2.5,
            tokens=tokens,
            name="attend_weights",
        )

    def end_back(layer, dmid, x, terms, tokens=()):
        return call(
            functools.partial(end_bwd_body, 3),
            [((rows, width), BF), ((2, width), F32)],
            [dmid, x, vec[layer], *terms],
            tokens=tokens,
            name="end_bwd",
        )

    up1, (du, small_up1) = feed_back(g1, wfeed1, feed1)
    keep_a, keep_b, send_a, send_b = feed_weights(c1, g1, feed1, du)
    dmid1, dlow, small_mid1 = mid_back(1, grad1, mid1, scatter_rel(up1)[0], [keep_a])
    came_a, came_b = swap_micro(send_a), swap_micro(send_b)
    hb1 = gather_rel(dlow, [came_a])
    far, near = swap_rank(down1[3], 2), swap_rank(down1[2], 2)
    (chip,) = call(
        total_body, [((rows, width), BF)], [down1[1], far], tokens=[hb1[1]], name="chip_sum"
    )
    mine_a, send_a = split_dp(keep_a, came_a, 1, meta)
    in1, (dq, dk, dv, small_qv1) = attend_back(hb1, wattend1, att1, [chip, mine_a])
    came_a = swap_level(send_a, 1)
    (x2,) = call(
        functools.partial(last_fwd_body, 3),
        [((rows, width), BF)],
        [mid1, vec[1], down1[0], near, swap_rank(chip, 1)],
        tokens=[in1[0]],
        name="last_fwd",
    )
    terms, chip = scatter_rel(in1, [came_b, came_a])
    mine_b, send_b = split_dp(keep_b, came_b, 1, meta, [chip])
    came_b = swap_level(send_b, 1)
    keep, send = attend_weights(a1, hb1, att1, (dq, dk, dv), [chip])
    dx1, small_end1 = end_back(1, dmid1, x1, terms, [keep, came_b, x2])
    came = swap_micro(send)
    mine_a, send_a = split_dp(mine_a, came_a, 0, meta, [dx1])
    mine_b, send_b = split_dp(mine_b, came_b, 0, meta, [dx1])
    came_a, came_b = swap_level(send_a, 0), swap_level(send_b, 0)
    g0 = gather_rel(dx1, [came, came_a, came_b])
    mine, send = split_dp(keep, came, 1, meta)
    gfeed1a, gfeed1b = add(mine_a, came_a), add(mine_b, came_b)

    up0, (du, small_up0) = feed_back(g0, wfeed0, feed0, [mine, gfeed1a, gfeed1b])
    came = swap_level(send, 1)
    keep_a, keep_b, send_a, send_b = feed_weights(c0, g0, feed0, du)
    dmid0, dlow, small_mid0 = mid_back(0, dx1, mid0, scatter_rel(up0)[0], [keep_a, came])
    mine, send = split_dp(mine, came, 0, meta, [dlow])
    came = swap_level(send, 0)
    came_a, came_b = swap_micro(send_a), swap_micro(send_b)
    hb0 = gather_rel(dlow, [came_a, came])
    gattend1 = add(mine, came)
    mine_a, send_a = split_dp(keep_a, came_a, 1, meta)
    late = gate(x2, [mine_a])
    in0, (dq, dk, dv, small_qv0) = attend_back(hb0, wattend0, att0, [mine_a, gattend1])
    layer_out = collect(x1, late, [in0[0]])
    came_a = swap_level(send_a, 1)
    terms, chip = scatter_rel(in0, [came_b, came_a])
    mine_b, send_b = split_dp(keep_b, came_b, 1, meta, [chip])
    mine_a, send_a = split_dp(mine_a, came_a, 0, meta, [chip])
    came_a, came_b = swap_level(send_a, 0), swap_level(send_b, 1)
    keep, send = attend_weights(a0, hb0, att0, (dq, dk, dv), [chip, layer_out])
    blocks = pair_sum(keep, swap_micro(send), meta)
    dx0, small_end0 = end_back(0, dmid0, x0, terms, [blocks[0]])
    gfeed0a = add(mine_a, came_a)
    mine_b, send_b = split_dp(mine_b, came_b, 0, meta, [dx0])
    gfeed0b = add(mine_b, swap_level(send_b, 0))
    gattend0 = sum_blocks(blocks)
    whole = sum_ranks(
        jnp.concatenate([small_end0, small_mid0, small_end1, small_mid1], axis=0)
    )
    whole = [whole[:6], pad(small_up0), pad(small_qv0), whole[6:], pad(small_up1), pad(small_qv1)]
    whole = sum_dp(jnp.concatenate(whole, axis=0))
    small0, small1 = whole[:8], whole[8:]

    def to_owner(first, second):
        return [leave_seat(t, flip) for flip, t in enumerate(pick(first, second))]

    gfeed0 = jnp.concatenate([gfeed0a, gfeed0b], axis=1)
    gfeed1 = jnp.concatenate([gfeed1a, gfeed1b], axis=1)
    count = gfeed0.shape[0]
    gup, gdown = call(
        finish_feed_body,
        [((count, units), F32), ((units, count), F32)],
        to_owner(gfeed0, gfeed1),
        scalars=meta,
        name="finish_feed",
    )
    gqkv, gout = call(
        finish_attend_body,
        [((3, count, heads), F32), ((heads, count), F32)],
        to_owner(gattend0, gattend1),
        scalars=meta,
        name="finish_attend",
    )
    input_grad = collect(dx0, dx1)

    mine = sum(leave_seat(t, flip) for flip, t in enumerate(pick(small0, small1)))
    return (
        layer_out,
        input_grad,
        jnp.stack([mine[0], mine[2]])[None],
        jnp.stack([mine[1], mine[3]])[None],
        gqkv[None],
        mine[7, : 2 * heads].reshape(1, 2, heads),
        gout[None],
        mine[4][None],
        gup[None],
        mine[6, :units][None],
        gdown[None],
        mine[5][None],
    )


def solution(mesh):
    in_specs = (
        P(None, ("dp", "tensor"), None),
        P(None, ("dp", "tensor"), None),
        P(None, "dp", None),
        P("section", None, None),
        P("section", None, None),
        P("section", None, "dp", "tensor"),
        P("section", None, "tensor"),
        P("section", "tensor", "dp"),
        P("section", None),
        P("section", "dp", "tensor"),
        P("section", "tensor"),
        P("section", "tensor", "dp"),
        P("section", None),
    )
    out_specs = (
        P("section", None, ("dp", "tensor"), None),
        P("section", None, ("dp", "tensor"), None),
        P("section", None, None),
        P("section", None, None),
        P("section", None, "dp", "tensor"),
        P("section", None, "tensor"),
        P("section", "tensor", "dp"),
        P("section", None),
        P("section", "dp", "tensor"),
        P("section", "tensor"),
        P("section", "tensor", "dp"),
        P("section", None),
    )
    return jax.shard_map(shards, mesh=mesh, in_specs=in_specs, out_specs=out_specs, check_vma=False)
```

```python
import functools

import jax
import jax.numpy as jnp
from jax import lax
from jax.experimental import pallas as pl
from jax.experimental.pallas import tpu as pltpu
from jax.sharding import PartitionSpec as P

HD = 64
BF = jnp.bfloat16
F32 = jnp.float32
VMEM = pl.BlockSpec(memory_space=pltpu.VMEM)
SMEM = pl.BlockSpec(memory_space=pltpu.SMEM)
MIB = 1 << 20

RANK, MICRO, DP, LAST, HALF, META = range(6)

GAIN0, GAIN1, SHIFT0, SHIFT1, B_OUT, B_DOWN, B_UP, B_QV = range(8)


def nn(left, right):
    return lax.dot_general(left, right, (((1,), (0,)), ((), ())), preferred_element_type=F32)


def nt(left, right):
    return lax.dot_general(left, right, (((1,), (1,)), ((), ())), preferred_element_type=F32)


def tn(left, right):
    return lax.dot_general(left, right, (((0,), (0,)), ((), ())), preferred_element_type=F32)


def call(
    body, outs, args, scalars=None, tokens=(), scratch=(), vmem=12, name=None, us=0.5
):
    args = ([] if scalars is None else [scalars]) + list(args)
    count = len(args)

    def kernel(*refs):
        body(*refs[:count], *refs[count + len(tokens) :])

    return pl.pallas_call(
        kernel,
        out_shape=[jax.ShapeDtypeStruct(s, d) for s, d in outs],
        in_specs=([] if scalars is None else [SMEM])
        + [VMEM] * (count - (scalars is not None))
        + [pl.BlockSpec(memory_space=pl.ANY)] * len(tokens),
        out_specs=[VMEM] * len(outs),
        scratch_shapes=list(scratch),
        compiler_params=pltpu.CompilerParams(vmem_limit_bytes=vmem * MIB),
        cost_estimate=pl.CostEstimate(flops=int(us * 1.15e9), bytes_accessed=1, transcendentals=0),
        name=name,
    )(*args, *tokens)


def swap(value, axis, by):
    count = lax.axis_size(axis)
    return lax.ppermute(value, axis, [(i, i ^ by) for i in range(count)])


def seat(micro, rank):
    half = lax.axis_size("tensor") // 2
    return rank // half * 2 * half + micro * half + rank % half


def permute(value, pairs):
    return lax.ppermute(value, ("section", "tensor"), pairs)


def seats():
    return [(m, r) for m in range(2) for r in range(lax.axis_size("tensor"))]


def swap_micro(value):
    return permute(value, [(seat(m, r), seat(1 - m, r)) for m, r in seats()])


def swap_rank(value, by):
    return permute(value, [(seat(m, r), seat(m, r ^ by)) for m, r in seats()])


def take_seat(value, flip):
    count = lax.axis_size("tensor")
    return permute(value, [((m ^ flip) * count + r, seat(m, r)) for m, r in seats()])


def leave_seat(value, flip):
    count = lax.axis_size("tensor")
    return permute(value, [(seat(m, r), (m ^ flip) * count + r) for m, r in seats()])


def gate(value, tokens):
    if not tokens:
        return value
    anywhere = pl.BlockSpec(memory_space=pl.ANY)

    def kernel(*refs):
        pass

    return pl.pallas_call(
        kernel,
        out_shape=jax.ShapeDtypeStruct(value.shape, value.dtype),
        in_specs=[anywhere] * (1 + len(tokens)),
        out_specs=anywhere,
        input_output_aliases={0: 0},
        compiler_params=pltpu.CompilerParams(vmem_limit_bytes=MIB),
        cost_estimate=pl.CostEstimate(flops=1, bytes_accessed=1, transcendentals=0),
        name="gate",
    )(value, *tokens)


def gather_rel(own, tokens=()):
    chip = gate(swap_rank(own, 1), tokens)
    return [own, chip, swap_rank(own, 2), swap_rank(chip, 2)]


def scatter_rel(parts, tokens=()):
    far = swap_rank(gate(parts[3], tokens), 2)
    near = swap_rank(parts[2], 2)
    (chip,) = call(total_body, [(far.shape, BF)], [parts[1], far], name="chip_sum")
    return [parts[0], near, swap_rank(chip, 1)], chip


def row_norm(x):
    mean = jnp.mean(x, axis=-1, keepdims=True)
    centred = x - mean
    var = jnp.mean(centred * centred, axis=-1, keepdims=True)
    inv = lax.rsqrt(var + 1e-05)
    return centred * inv, inv


def norm_back(grad, xhat, inv, gain):
    gx = grad * gain
    m1 = jnp.mean(gx, axis=-1, keepdims=True)
    m2 = jnp.mean(gx * xhat, axis=-1, keepdims=True)
    return inv * (gx - m1 - xhat * m2)


def add_terms(refs):
    total = refs[0][...].astype(F32)
    for ref in refs[1:]:
        total = total + ref[...].astype(F32)
    return total


def first_norm_body(x, vec, out):
    xhat, _ = row_norm(x[...].astype(F32))
    out[...] = (xhat * vec[GAIN0 : GAIN0 + 1, :] + vec[SHIFT0 : SHIFT0 + 1, :]).astype(BF)


def mid_fwd_body(parts, *refs):
    x, vec = refs[:2]
    terms = refs[2 : 2 + parts]
    mid, out = refs[2 + parts :]
    h = x[...].astype(F32) + add_terms(terms) + vec[B_OUT : B_OUT + 1, :]
    mid[...] = h
    xhat, _ = row_norm(h)
    out[...] = (xhat * vec[GAIN1 : GAIN1 + 1, :] + vec[SHIFT1 : SHIFT1 + 1, :]).astype(BF)


def end_fwd_body(parts, *refs):
    mid, vec, vec_next = refs[:3]
    terms = refs[3 : 3 + parts]
    result, out = refs[3 + parts :]
    y = (mid[...] + add_terms(terms) + vec[B_DOWN : B_DOWN + 1, :]).astype(BF)
    result[...] = y
    xhat, _ = row_norm(y.astype(F32))
    out[...] = (xhat * vec_next[GAIN0 : GAIN0 + 1, :] + vec_next[SHIFT0 : SHIFT0 + 1, :]).astype(BF)


def last_fwd_body(parts, *refs):
    mid, vec = refs[:2]
    terms = refs[2 : 2 + parts]
    (result,) = refs[2 + parts :]
    result[...] = (mid[...] + add_terms(terms) + vec[B_DOWN : B_DOWN + 1, :]).astype(BF)


def mid_bwd_body(parts, *refs):
    g, mid, vec = refs[:3]
    terms = refs[3 : 3 + parts]
    grad_mid, grad_low, small = refs[3 + parts :]
    grad = g[...].astype(F32)
    back = add_terms(terms)
    xhat, inv = row_norm(mid[...])
    dh = grad + norm_back(back, xhat, inv, vec[GAIN1 : GAIN1 + 1, :])
    grad_mid[...] = dh
    grad_low[...] = dh.astype(BF)
    small[0:1, :] = jnp.sum(back * xhat, axis=0, keepdims=True)
    small[1:2, :] = jnp.sum(back, axis=0, keepdims=True)
    small[2:3, :] = jnp.sum(dh, axis=0, keepdims=True)
    small[3:4, :] = jnp.sum(grad, axis=0, keepdims=True)


def end_bwd_body(parts, *refs):
    grad_mid, x, vec = refs[:3]
    terms = refs[3 : 3 + parts]
    result, small = refs[3 + parts :]
    back = add_terms(terms)
    xhat, inv = row_norm(x[...].astype(F32))
    result[...] = (grad_mid[...] + norm_back(back, xhat, inv, vec[GAIN0 : GAIN0 + 1, :])).astype(BF)
    small[0:1, :] = jnp.sum(back * xhat, axis=0, keepdims=True)
    small[1:2, :] = jnp.sum(back, axis=0, keepdims=True)


def chosen(flag, first, second):
    return jnp.where(flag == 0, first[...], second[...])


def ordered_rows(rank, by, block):
    return pl.ds(pl.multiple_of((rank ^ by) * block, 8), block)


def strip_mask(meta, slots, first, rows, cols):
    place = first + lax.broadcasted_iota(jnp.int32, (rows, 1), 0)
    start = jnp.zeros((rows, 1), jnp.int32)
    for s in range(slots):
        end = meta[META + s]
        start = jnp.where(place >= end, end, start)
    start = jnp.where(place >= meta[META + slots - 1], place, start)
    key = lax.broadcasted_iota(jnp.int32, (rows, cols), 1)
    return (key >= start) & (key <= place)


def attend_fwd_body(parts, slots, *refs):
    meta, own_w, other_w, vec = refs[:4]
    pieces = refs[4 : 4 + parts]
    outs = refs[4 + parts : 4 + 2 * parts]
    q, k, v, o, stat = refs[4 + 2 * parts :]
    rank = meta[RANK]
    block, width = pieces[0].shape[0], own_w.shape[1] // 2
    wqk = chosen(meta[MICRO], own_w, other_w)
    wvo = chosen(meta[MICRO], other_w, own_w)
    wq, wk, wv, wout = wqk[:, :width], wqk[:, width:], wvo[:, :width], wvo[:, width:]
    qb = vec[B_QV : B_QV + 1, :width]
    vb = vec[B_QV : B_QV + 1, width : 2 * width]
    for j in range(parts):
        rows = ordered_rows(rank, j, block)
        a = pieces[j][...]
        q[rows, :] = ((nn(a, wq) + qb) * (HD**-0.5)).astype(BF)
        k[rows, :] = nn(a, wk).astype(BF)
        v[rows, :] = (nn(a, wv) + vb).astype(BF)
    for i in range(parts):
        rows, cols = slice(i * block, (i + 1) * block), (i + 1) * block
        mask = strip_mask(meta, slots, i * block, block, cols)
        lane = lax.broadcasted_iota(jnp.int32, (block, 128), 1)
        stats = jnp.zeros((block, 128), F32)
        for h in range(width // HD):
            own = slice(h * HD, (h + 1) * HD)
            s = jnp.where(mask, nt(q[rows, own], k[:cols, own]), -1e9)
            top = jnp.max(s, axis=-1, keepdims=True)
            e = jnp.exp(s - top)
            total = jnp.sum(e, axis=-1, keepdims=True)
            p = (e * (1.0 / total)).astype(BF)
            o[rows, own] = nn(p, v[:cols, own]).astype(BF)
            stats = jnp.where(lane == h, top + jnp.log(total), stats)
        stat[rows, :] = stats
    for j in range(parts):
        outs[j][...] = nt(o[ordered_rows(rank, j, block), :], wout).astype(BF)


def attend_bwd_body(parts, slots, *refs):
    meta, own_w, other_w, q, k, v, stat = refs[:7]
    pieces = refs[7 : 7 + parts]
    outs = refs[7 + parts : 7 + 2 * parts]
    dq, dk, dv, small, do, dkf, dvf = refs[7 + 2 * parts :]
    rank = meta[RANK]
    block, width = pieces[0].shape[0], own_w.shape[1] // 2
    wqk = chosen(meta[MICRO], own_w, other_w)
    wvo = chosen(meta[MICRO], other_w, own_w)
    wq, wk, wv, wout = wqk[:, :width], wqk[:, width:], wvo[:, :width], wvo[:, width:]
    for j in range(parts):
        do[ordered_rows(rank, j, block), :] = nn(pieces[j][...], wout).astype(BF)
    for i in reversed(range(parts)):
        rows, cols = slice(i * block, (i + 1) * block), (i + 1) * block
        mask = strip_mask(meta, slots, i * block, block, cols)
        for h in range(width // HD):
            own = slice(h * HD, (h + 1) * HD)
            qh, kh, vh, doh = q[rows, own], k[:cols, own], v[:cols, own], do[rows, own]
            s = jnp.where(mask, nt(qh, kh), -1e9)
            p = jnp.exp(s - stat[rows, h : h + 1])
            dp = nt(doh, vh)
            inner = jnp.sum(dp * p, axis=-1, keepdims=True)
            ds = (p * (dp - inner)).astype(BF)
            dq[rows, own] = (nn(ds, kh).astype(BF).astype(F32) * (HD**-0.5)).astype(BF)
            dkh, dvh = tn(ds, qh), tn(p.astype(BF), doh)
            if i == parts - 1:
                dkf[h] = dkh
                dvf[h] = dvh
            else:
                dkf[h, :cols] += dkh
                dvf[h, :cols] += dvh
    for h in range(width // HD):
        own = slice(h * HD, (h + 1) * HD)
        dk[:, own] = dkf[h].astype(BF)
        dv[:, own] = dvf[h].astype(BF)
    small[0:1, :] = jnp.sum(dq[...].astype(F32), axis=0, keepdims=True)
    small[1:2, :] = jnp.sum(dv[...].astype(F32), axis=0, keepdims=True)
    for j in range(parts):
        rows = ordered_rows(rank, j, block)
        outs[j][...] = (nt(dq[rows, :], wq) + nt(dk[rows, :], wk) + nt(dv[rows, :], wv)).astype(BF)


def attend_weights_body(parts, *refs):
    meta, o, dq, dk, dv = refs[:5]
    normed = refs[5 : 5 + parts]
    grads = refs[5 + parts : 5 + 2 * parts]
    keep, send = refs[5 + 2 * parts :]
    rank, flag = meta[RANK], meta[MICRO]
    block, width = normed[0].shape[0], o.shape[1]
    totals = [None] * 4
    for j in range(parts):
        rows = ordered_rows(rank, j, block)
        a, g = normed[j][...], grads[j][...]
        terms = [tn(a, dq[rows, :]), tn(a, dk[rows, :]), tn(a, dv[rows, :]), tn(g, o[rows, :])]
        totals = [t if s is None else s + t for s, t in zip(totals, terms)]
    q, k, v, out = [t.astype(BF) for t in totals]
    keep[:, :width] = jnp.where(flag == 0, q, v)
    keep[:, width:] = jnp.where(flag == 0, k, out)
    send[:, :width] = jnp.where(flag == 0, v, q)
    send[:, width:] = jnp.where(flag == 0, out, k)


def feed_fwd_body(parts, *refs):
    meta, own_w, other_w, vec = refs[:4]
    pieces = refs[4 : 4 + parts]
    outs = refs[4 + parts : 4 + 2 * parts]
    hidden, slope = refs[4 + 2 * parts :]
    block = pieces[0].shape[0]
    wup = chosen(meta[MICRO], own_w, other_w)
    wdown = chosen(meta[MICRO], other_w, own_w)
    bias = vec[B_UP : B_UP + 1, : wup.shape[1]]
    for j in range(parts):
        rows = slice(j * block, (j + 1) * block)
        u = nn(pieces[j][...], wup) + bias
        share = 0.5 * (1.0 + lax.erf(u * (0.5**0.5)))
        f = (u * share).astype(BF)
        hidden[rows, :] = f
        slope[rows, :] = (share + u * (jnp.exp(-0.5 * (u * u)) * 0.3989422804014327)).astype(BF)
        outs[j][...] = nt(f, wdown).astype(BF)


def feed_bwd_body(parts, *refs):
    meta, own_w, other_w, slope = refs[:4]
    pieces = refs[4 : 4 + parts]
    outs = refs[4 + parts : 4 + 2 * parts]
    du, small = refs[4 + 2 * parts :]
    block = pieces[0].shape[0]
    wup = chosen(meta[MICRO], own_w, other_w)
    wdown = chosen(meta[MICRO], other_w, own_w)
    total = None
    for j in range(parts):
        rows = slice(j * block, (j + 1) * block)
        d = (nn(pieces[j][...], wdown) * slope[rows, :].astype(F32)).astype(BF)
        du[rows, :] = d
        term = jnp.sum(d.astype(F32), axis=0, keepdims=True)
        total = term if total is None else total + term
        outs[j][...] = nt(d, wup).astype(BF)
    small[...] = total


def feed_weights_body(parts, *refs):
    meta, hidden, du = refs[:3]
    normed = refs[3 : 3 + parts]
    grads = refs[3 + parts : 3 + 2 * parts]
    keep_a, keep_b, send_a, send_b = refs[3 + 2 * parts :]
    flag = meta[MICRO]
    block, half = normed[0].shape[0], keep_a.shape[1]
    up = down = None
    for j in range(parts):
        rows = slice(j * block, (j + 1) * block)
        t_up, t_down = tn(normed[j][...], du[rows, :]), tn(grads[j][...], hidden[rows, :])
        up, down = (t_up, t_down) if up is None else (up + t_up, down + t_down)
    up, down = up.astype(BF), down.astype(BF)
    keep_a[...] = jnp.where(flag == 0, up[:, :half], down[:, :half])
    keep_b[...] = jnp.where(flag == 0, up[:, half:], down[:, half:])
    send_a[...] = jnp.where(flag == 0, down[:, :half], up[:, :half])
    send_b[...] = jnp.where(flag == 0, down[:, half:], up[:, half:])


def layer_slice_body(layer, meta, own, other, out):
    out[...] = chosen(meta[MICRO] ^ layer, own, other)


def masked_body(meta, x, out):
    rows = x.shape[0]
    place = meta[RANK] * rows + lax.broadcasted_iota(jnp.int32, (rows, 1), 0)
    out[...] = jnp.where(place < meta[LAST], x[...].astype(F32), 0.0).astype(BF)


def assemble_body(meta, *refs):
    pieces, out = refs[:-1], refs[-1]
    size = pieces[0].shape[0]
    for k, piece in enumerate(pieces):
        out[ordered_rows(meta[DP], k, size), :] = piece[...]


def bit_of(meta, level):
    return (meta[DP] >> level) & 1


def join_body(level, meta, own, came, out):
    size = own.shape[0]
    bit = bit_of(meta, level)
    out[pl.ds(pl.multiple_of(bit * size, 8), size), :] = own[...]
    out[pl.ds(pl.multiple_of((1 - bit) * size, 8), size), :] = came[...]


def split_sum_body(level, meta, first, second, mine, send):
    size = mine.shape[0]
    bit = bit_of(meta, level)
    for part, out in ((bit, mine), (1 - bit, send)):
        rows = pl.ds(pl.multiple_of(part * size, 8), size)
        out[...] = (first[rows, :].astype(F32) + second[rows, :].astype(F32)).astype(out.dtype)


def pair_sum_body(meta, keep, came, *outs):
    size = outs[0].shape[0]
    for k, out in enumerate(outs):
        rows = ordered_rows(meta[DP], k, size)
        out[...] = (keep[rows, :].astype(F32) + came[rows, :].astype(F32)).astype(out.dtype)


def collect_body(meta, own, other, out):
    flag = jnp.where(meta[RANK] < meta[HALF], 0, 1)
    out[0] = chosen(flag, own, other)
    out[1] = chosen(flag, other, own)


def finish_feed_body(meta, own, other, up, down):
    flag = jnp.where(meta[RANK] < meta[HALF], 0, 1)
    up[...] = chosen(flag, own, other).astype(F32)
    down[...] = chosen(flag, other, own).astype(F32).T


def finish_attend_body(meta, own, other, qkv, out):
    flag = jnp.where(meta[RANK] < meta[HALF], 0, 1)
    width = out.shape[0]
    first = chosen(flag, own, other).astype(F32)
    second = chosen(flag, other, own).astype(F32)
    qkv[0] = first[:, :width]
    qkv[1] = first[:, width:]
    qkv[2] = second[:, :width]
    out[...] = second[:, width:].T


def total_body(*refs):
    refs[-1][...] = add_terms(refs[:-1]).astype(refs[-1].dtype)


def gather_dp(shard, meta, tokens=()):
    count = lax.axis_size("dp")
    if count > 8:
        return lax.all_gather(shard, "dp", axis=0, tiled=True), shard
    pieces = [shard] + [swap(shard, "dp", k) for k in range(1, count)]
    shape = (shard.shape[0] * count, shard.shape[1])
    (whole,) = call(assemble_body, [(shape, BF)], pieces, scalars=meta, tokens=tokens, name="assemble")
    return whole, pieces[1]


def pair_sum(keep, came, meta, tokens=()):
    count = lax.axis_size("dp")
    if count > 8:
        return [(keep.astype(F32) + came.astype(F32)).astype(BF)]
    shape = (keep.shape[0] // count, keep.shape[1])
    return call(
        pair_sum_body,
        [(shape, F32)] + [(shape, BF)] * (count - 1),
        [keep, came],
        scalars=meta,
        tokens=tokens,
        name="pair_sum",
    )


def sum_blocks(blocks, tokens=()):
    if len(blocks) == 1:
        return lax.psum_scatter(blocks[0], "dp", scatter_dimension=0, tiled=True)
    terms = [blocks[0]] + [swap(blocks[k], "dp", k) for k in range(1, len(blocks))]
    (total,) = call(total_body, [(blocks[0].shape, BF)], terms, tokens=tokens, name="total")
    return total


def join_dp(shard, level, meta, tokens=()):
    if lax.axis_size("dp") != 4:
        return lax.all_gather(shard, "dp", axis=0, tiled=True) if level else shard
    came = swap(shard, "dp", 1 << level)
    shape = (2 * shard.shape[0], shard.shape[1])
    (out,) = call(
        functools.partial(join_body, level),
        [(shape, BF)],
        [shard, came],
        scalars=meta,
        tokens=tokens,
        name="join",
    )
    return out


def split_dp(first, second, level, meta, tokens=()):
    if lax.axis_size("dp") != 4:
        both = first.astype(F32) + second.astype(F32)
        if level == 0:
            return both, jnp.zeros_like(both)
        both = lax.psum_scatter(both.astype(BF), "dp", scatter_dimension=0, tiled=True)
        return both, jnp.zeros_like(both)
    shape = (first.shape[0] // 2, first.shape[1])
    return call(
        functools.partial(split_sum_body, level),
        [(shape, F32), (shape, BF)],
        [first, second],
        scalars=meta,
        tokens=tokens,
        name="split_sum",
    )


def swap_level(value, level):
    return swap(value, "dp", 1 << level)


def add(first, second, tokens=()):
    (out,) = call(total_body, [(first.shape, BF)], [first, second], tokens=tokens, name="total")
    return out


def sum_dp(value, tokens=()):
    count = lax.axis_size("dp")
    if count > 8:
        return lax.psum(value, "dp")
    by = 1
    while by < count:
        terms = [value, swap(value, "dp", by)]
        (value,) = call(total_body, [(value.shape, F32)], terms, tokens=tokens, name="sum_dp")
        by *= 2
    return value


def sum_ranks(value, tokens=()):
    by = 1
    while by < lax.axis_size("tensor"):
        terms = [value, swap_rank(value, by)]
        (value,) = call(total_body, [(value.shape, F32)], terms, tokens=tokens, name="sum_ranks")
        by *= 2
    return value


def shards(
    inputs,
    cotangent,
    seq_lengths,
    norm_gain,
    norm_shift,
    w_qkv,
    b_qv,
    w_out,
    b_out,
    w_up,
    b_up,
    w_down,
    b_down,
):
    parts = lax.axis_size("tensor")
    section, place = lax.axis_index("section"), lax.axis_index("tensor")
    micro = place // (parts // 2)
    rank = section * (parts // 2) + place % (parts // 2)
    own_first = micro == 0
    rows, width = inputs.shape[1], inputs.shape[2]
    total_rows = rows * parts
    slots = seq_lengths.shape[2]
    heads = w_qkv.shape[3]
    units = w_up.shape[2]

    def by_layer(own, other):
        return jnp.where(own_first, own, other), jnp.where(own_first, other, own)

    def pad(row):
        return jnp.pad(row.reshape(1, -1), ((0, 0), (0, width - row.size)))

    lengths = lax.dynamic_index_in_dim(seq_lengths[:, 0], micro, 0, keepdims=False)
    ends = jnp.cumsum(lengths).astype(jnp.int32)
    meta = [rank, micro, lax.axis_index("dp"), ends[-1], parts // 2]
    meta = jnp.stack([jnp.asarray(m, jnp.int32) for m in meta])
    meta = jnp.concatenate([meta, ends])
    block_out = [((rows, width), BF)] * parts
    tall = ((total_rows, heads), BF)

    def slices_of(first, second, tokens=()):
        own, other = jnp.where(section == 0, first, second), jnp.where(section == 0, second, first)
        own, other = take_seat(gate(own, tokens), 0), take_seat(gate(other, tokens), 1)
        return own, other

    def layer_slice(slices, layer, tokens=()):
        (out,) = call(
            functools.partial(layer_slice_body, layer),
            [(slices[0].shape, BF)],
            slices,
            scalars=meta,
            tokens=tokens,
            name="layer_slice",
        )
        return out

    packed = jnp.concatenate(
        [norm_gain[0], norm_shift[0], b_out, b_down, pad(b_up[0]), pad(b_qv[0])], axis=0
    )
    attend_first = jnp.concatenate([w_qkv[0, 0], w_qkv[0, 1]], axis=1)
    attend_second = jnp.concatenate([w_qkv[0, 2], w_out[0].T], axis=1)
    attend_slices = slices_of(attend_first, attend_second)
    x0 = take_seat(lax.dynamic_index_in_dim(inputs, section, 0, keepdims=False), 0)
    vec = by_layer(take_seat(packed, 0), take_seat(packed, 1))
    attend_slice0 = layer_slice(attend_slices, 0, [x0, vec[0]])
    attend_own0, first_piece = gather_dp(attend_slice0, meta)
    (normed,) = call(first_norm_body, [((rows, width), BF)], [x0, vec[0]], name="norm_first")
    a0 = gather_rel(normed)
    feed_slices = slices_of(w_up[0], w_down[0].T, [first_piece])
    half = join_dp(layer_slice(feed_slices, 0, [attend_own0]), 0, meta)
    wattend0 = (attend_own0, swap_micro(attend_own0))

    def attend_fwd(layer, pieces, weights, tokens=()):
        res = call(
            functools.partial(attend_fwd_body, parts, slots),
            block_out + [tall, tall, tall, tall, ((total_rows, 128), F32)],
            [*weights, vec[layer], *pieces],
            scalars=meta,
            vmem=24,
            tokens=tokens,
            us=0.1,
            name="attend_fwd",
        )
        return res[:parts], res[parts:]

    def feed_fwd(layer, pieces, weights, tokens=()):
        res = call(
            functools.partial(feed_fwd_body, parts),
            block_out + [((total_rows, units), BF)] * 2,
            [*weights, vec[layer], *pieces],
            scalars=meta,
            vmem=24,
            tokens=tokens,
            us=0.1,
            name="feed_fwd",
        )
        return res[:parts], res[parts:]

    def mid_fwd(layer, x, terms, tokens=()):
        return call(
            functools.partial(mid_fwd_body, 3),
            [((rows, width), F32), ((rows, width), BF)],
            [x, vec[layer], *terms],
            tokens=tokens,
            name="mid_fwd",
        )

    out0, att0 = attend_fwd(0, a0, wattend0, [half])
    terms, chip = scatter_rel(out0)
    feed_own0 = join_dp(half, 1, meta, [chip])
    mid0, normed = mid_fwd(0, x0, terms, [feed_own0])
    wfeed0 = (feed_own0, swap_micro(feed_own0))
    half = join_dp(layer_slice(attend_slices, 1, [feed_own0]), 0, meta)
    c0 = gather_rel(normed, [half])
    down0, feed0 = feed_fwd(0, c0, wfeed0)
    attend_own1 = join_dp(half, 1, meta, [down0[0]])
    wattend1 = (attend_own1, swap_micro(attend_own1))
    half = join_dp(layer_slice(feed_slices, 1, [attend_own1]), 0, meta)
    x1, normed = call(
        functools.partial(end_fwd_body, 3),
        [((rows, width), BF), ((rows, width), BF)],
        [mid0, vec[0], vec[1], *scatter_rel(down0, [attend_own1])[0]],
        tokens=[half],
        name="end_fwd",
    )
    a1 = gather_rel(normed, [wattend1[1]])
    cot = lax.dynamic_index_in_dim(cotangent, section, 0, keepdims=False)
    cot = take_seat(gate(cot, [normed]), 0)
    (grad1,) = call(
        masked_body, [((rows, width), BF)], [cot], scalars=meta, tokens=[a1[1]], name="masked"
    )
    g1 = gather_rel(grad1)
    out1, att1 = attend_fwd(1, a1, wattend1, [grad1])
    feed_own1 = join_dp(half, 1, meta, [out1[0]])
    wfeed1 = (feed_own1, swap_micro(feed_own1))
    mid1, normed = mid_fwd(1, x1, scatter_rel(out1, [g1[1], feed_own1])[0])
    c1 = gather_rel(normed)
    down1, feed1 = feed_fwd(1, c1, wfeed1)

    def pick(first, second):
        return jnp.where(own_first, first, second), jnp.where(own_first, second, first)

    def collect(first, second, tokens=()):
        own, other = [leave_seat(t, flip) for flip, t in enumerate(pick(first, second))]
        (out,) = call(
            collect_body, [((2, rows, width), BF)], [own, other], scalars=meta, tokens=tokens, name="collect"
        )
        return out[None]

    def feed_back(g, weights, feed, tokens=()):
        res = call(
            functools.partial(feed_bwd_body, parts),
            block_out + [((total_rows, units), BF), ((1, units), F32)],
            [*weights, feed[1], *g],
            scalars=meta,
            vmem=24,
            tokens=tokens,
            us=3.5,
            name="feed_bwd",
        )
        return res[:parts], res[parts:]

    def feed_weights(c, g, feed, du):
        return call(
            functools.partial(feed_weights_body, parts),
            [((width, units // 2), BF)] * 4,
            [feed[0], du, *c, *g],
            scalars=meta,
            vmem=24,
            us=3.3,
            name="feed_weights",
        )

    def mid_back(layer, grad, mid, terms, tokens=()):
        return call(
            functools.partial(mid_bwd_body, 3),
            [((rows, width), F32), ((rows, width), BF), ((4, width), F32)],
            [grad, mid, vec[layer], *terms],
            tokens=tokens,
            name="mid_bwd",
        )

    def attend_back(hb, weights, att, tokens=()):
        res = call(
            functools.partial(attend_bwd_body, parts, slots),
            block_out + [tall, tall, tall, ((2, heads), F32)],
            [*weights, *att[:3], att[4], *hb],
            scalars=meta,
            scratch=[
                pltpu.VMEM((total_rows, heads), BF),
                pltpu.VMEM((heads // HD, total_rows, HD), F32),
                pltpu.VMEM((heads // HD, total_rows, HD), F32),
            ],
            vmem=24,
            tokens=tokens,
            us=0.1,
            name="attend_bwd",
        )
        return res[:parts], res[parts:]

    def attend_weights(a, hb, att, grads, tokens):
        return call(
            functools.partial(attend_weights_body, parts),
            [((width, 2 * heads), BF), ((width, 2 * heads), BF)],
            [att[3], *grads, *a, *hb],
            scalars=meta,
            vmem=24,
            us=2.5,
            tokens=tokens,
            name="attend_weights",
        )

    def end_back(layer, dmid, x, terms, tokens=()):
        return call(
            functools.partial(end_bwd_body, 3),
            [((rows, width), BF), ((2, width), F32)],
            [dmid, x, vec[layer], *terms],
            tokens=tokens,
            name="end_bwd",
        )

    up1, (du, small_up1) = feed_back(g1, wfeed1, feed1)
    keep_a, keep_b, send_a, send_b = feed_weights(c1, g1, feed1, du)
    dmid1, dlow, small_mid1 = mid_back(1, grad1, mid1, scatter_rel(up1)[0], [keep_a])
    came_a, came_b = swap_micro(send_a), swap_micro(send_b)
    hb1 = gather_rel(dlow, [came_a])
    far, near = swap_rank(down1[3], 2), swap_rank(down1[2], 2)
    (chip,) = call(
        total_body, [((rows, width), BF)], [down1[1], far], tokens=[hb1[1]], name="chip_sum"
    )
    mine_a, send_a = split_dp(keep_a, came_a, 1, meta)
    in1, (dq, dk, dv, small_qv1) = attend_back(hb1, wattend1, att1, [chip, mine_a])
    came_a = swap_level(send_a, 1)
    chip = swap_rank(chip, 1)
    (x2,) = call(
        functools.partial(last_fwd_body, 3),
        [((rows, width), BF)],
        [mid1, vec[1], down1[0], near, chip],
        tokens=[in1[0]],
        name="last_fwd",
    )
    terms, chip = scatter_rel(in1, [came_b, came_a, chip])
    mine_b, send_b = split_dp(keep_b, came_b, 1, meta)
    came_b = swap_level(send_b, 1)
    keep, send = attend_weights(a1, hb1, att1, (dq, dk, dv), [chip, mine_b])
    dx1, small_end1 = end_back(1, dmid1, x1, terms, [keep, came_b, x2])
    came = swap_micro(send)
    mine_a, send_a = split_dp(mine_a, came_a, 0, meta, [dx1])
    mine_b, send_b = split_dp(mine_b, came_b, 0, meta, [dx1])
    came_a, came_b = swap_level(send_a, 0), swap_level(send_b, 0)
    g0 = gather_rel(dx1, [came, came_a, came_b])
    mine, send = split_dp(keep, came, 1, meta)
    gfeed1a, gfeed1b = add(mine_a, came_a), add(mine_b, came_b)

    up0, (du, small_up0) = feed_back(g0, wfeed0, feed0, [mine, gfeed1a, gfeed1b])
    came = swap_level(send, 1)
    keep_a, keep_b, send_a, send_b = feed_weights(c0, g0, feed0, du)
    dmid0, dlow, small_mid0 = mid_back(0, dx1, mid0, scatter_rel(up0)[0], [keep_a, came])
    mine, send = split_dp(mine, came, 0, meta, [dlow])
    came = swap_level(send, 0)
    came_a, came_b = swap_micro(send_a), swap_micro(send_b)
    hb0 = gather_rel(dlow, [came_a, came])
    gattend1 = add(mine, came)
    mine_a, send_a = split_dp(keep_a, came_a, 1, meta)
    late = gate(x2, [mine_a])
    in0, (dq, dk, dv, small_qv0) = attend_back(hb0, wattend0, att0, [mine_a, gattend1])
    layer_out = collect(x1, late, [in0[0]])
    came_a = swap_level(send_a, 1)
    terms, chip = scatter_rel(in0, [came_b, came_a])
    mine_b, send_b = split_dp(keep_b, came_b, 1, meta, [chip])
    mine_a, send_a = split_dp(mine_a, came_a, 0, meta, [chip])
    came_a, came_b = swap_level(send_a, 0), swap_level(send_b, 1)
    keep, send = attend_weights(a0, hb0, att0, (dq, dk, dv), [chip, layer_out])
    blocks = pair_sum(keep, swap_micro(send), meta)
    dx0, small_end0 = end_back(0, dmid0, x0, terms, [blocks[0]])
    gfeed0a = add(mine_a, came_a)
    mine_b, send_b = split_dp(mine_b, came_b, 0, meta, [dx0])
    gfeed0b = add(mine_b, swap_level(send_b, 0))
    gattend0 = sum_blocks(blocks)
    whole = sum_ranks(
        jnp.concatenate([small_end0, small_mid0, small_end1, small_mid1], axis=0)
    )
    whole = [whole[:6], pad(small_up0), pad(small_qv0), whole[6:], pad(small_up1), pad(small_qv1)]
    whole = sum_dp(jnp.concatenate(whole, axis=0))
    small0, small1 = whole[:8], whole[8:]

    def to_owner(first, second):
        return [leave_seat(t, flip) for flip, t in enumerate(pick(first, second))]

    gfeed0 = jnp.concatenate([gfeed0a, gfeed0b], axis=1)
    gfeed1 = jnp.concatenate([gfeed1a, gfeed1b], axis=1)
    count = gfeed0.shape[0]
    gup, gdown = call(
        finish_feed_body,
        [((count, units), F32), ((units, count), F32)],
        to_owner(gfeed0, gfeed1),
        scalars=meta,
        name="finish_feed",
    )
    gqkv, gout = call(
        finish_attend_body,
        [((3, count, heads), F32), ((heads, count), F32)],
        to_owner(gattend0, gattend1),
        scalars=meta,
        name="finish_attend",
    )
    input_grad = collect(dx0, dx1)

    mine = sum(leave_seat(t, flip) for flip, t in enumerate(pick(small0, small1)))
    return (
        layer_out,
        input_grad,
        jnp.stack([mine[0], mine[2]])[None],
        jnp.stack([mine[1], mine[3]])[None],
        gqkv[None],
        mine[7, : 2 * heads].reshape(1, 2, heads),
        gout[None],
        mine[4][None],
        gup[None],
        mine[6, :units][None],
        gdown[None],
        mine[5][None],
    )


def solution(mesh):
    in_specs = (
        P(None, ("dp", "tensor"), None),
        P(None, ("dp", "tensor"), None),
        P(None, "dp", None),
        P("section", None, None),
        P("section", None, None),
        P("section", None, "dp", "tensor"),
        P("section", None, "tensor"),
        P("section", "tensor", "dp"),
        P("section", None),
        P("section", "dp", "tensor"),
        P("section", "tensor"),
        P("section", "tensor", "dp"),
        P("section", None),
    )
    out_specs = (
        P("section", None, ("dp", "tensor"), None),
        P("section", None, ("dp", "tensor"), None),
        P("section", None, None),
        P("section", None, None),
        P("section", None, "dp", "tensor"),
        P("section", None, "tensor"),
        P("section", "tensor", "dp"),
        P("section", None),
        P("section", "dp", "tensor"),
        P("section", "tensor"),
        P("section", "tensor", "dp"),
        P("section", None),
    )
    return jax.shard_map(shards, mesh=mesh, in_specs=in_specs, out_specs=out_specs, check_vma=False)
```
